512 devices in a mesh: space: 64 (over y, z_lo, core), eig: 8 (over x, z_hi).
Axes of the slice: x: 4, y: 8, z: 8 (z_hi: 2, z_lo: 4; z = z_hi * 4 + z_lo), core: 2. Of those that a mesh axis runs over, the one named last changes fastest.
Arguments:
- eigenvectors: bfloat16 [256, 3, 2, 64, 512], P('eig', None, None, 'space'), may hold values from -2.5 to 2.5
- gauge_links: float32 [3, 3, 3, 2, 64, 512], P(None, None, None, None, 'space'), may hold values from -6 to 6
- momenta: int32 [4, 3], replicated, may hold values from -2 to 2
Outputs:
- elementals: float32 [3, 4, 2, 256, 256], P(None, None, None, 'eig', 'space')
The draws below stay inside these ranges and needn't reach their ends.
All inputs are finite; a program needn't handle non-finite values.
Results may differ from the reference program's by a relative error of at most 0.0029.
Values may be sent and summed in bfloat16 or wider, within the bound.
No kernel may reach another device: no remote copies, remote signals or barrier semaphores. Data moves between devices by JAX's collectives and lax.ppermute only.
A program may use at most 64 MiB of HBM per device.

```python
import math
import jax
import jax.numpy as jnp
from jax import lax

NEV = 256
NMOM = 4
NDISP = 3
LX = 64
LY = 8
NZ = 64


def plant(drawn, key, least, top_value):
    index_at = [jax.random.randint(jax.random.fold_in(key, axis), (), 0, length) for axis, length in enumerate(drawn.shape)]
    widest = drawn.shape.index(max(drawn.shape))
    next_to = index_at[:widest] + [(index_at[widest] + 1) % drawn.shape[widest]] + index_at[widest + 1:]
    return drawn.at[tuple(index_at)].set(least).at[tuple(next_to)].set(top_value)


def strengthened(entries, key, source, target, shards_of, factor):
    def block_of(position):
        return (jnp.arange(entries.shape[position]) // (entries.shape[position] // shards_of)).reshape((-1,) + (1,) * (entries.ndim - 1 - position))

    near = jax.random.permutation(key, shards_of)[block_of(target)]
    other_side = (block_of(target) + shards_of // 2) % shards_of
    return jnp.where((block_of(source) == near) | (block_of(source) == other_side), factor * entries, entries)


def level_of(key, dims, pieces, low, high):
    level, own = 1.0, jax.random.fold_in(key, 6)
    for position, blocks in pieces:
        steps = jnp.exp(jax.random.uniform(jax.random.fold_in(own, position), (blocks,), jnp.float32, low / len(pieces), high / len(pieces)))
        level = level * jnp.repeat(steps, dims[position] // blocks).reshape([-1 if axis == position else 1 for axis in range(len(dims))])
    return level


def centred(key, shape, width, most, cuts=(), kind=jnp.bfloat16):
    loudness = level_of(key, shape, cuts, -0.22, 0.18) if cuts else 1.0
    drawn = jax.random.normal(key, shape, jnp.float32) * width * loudness
    return jnp.minimum(jnp.maximum(drawn, -most), most).astype(kind)


def bell_draw_with(rng, shape, spread, limit, split, heavy, held_as=jnp.bfloat16):
    values = spread * jax.random.normal(rng, shape, jnp.float32)
    if split:
        values = values * level_of(rng, shape, split, -0.22, 0.18)
    return jnp.clip(strengthened(values, jax.random.fold_in(rng, 3), *heavy), -limit, limit).astype(held_as)


def setup_inputs(seed: int = 0) -> dict:
    streams_of = jax.random.split(jax.random.key(seed), 4)
    eigenvectors = bell_draw_with(streams_of[0], (NEV, 3, 2, NZ, LY * LX), ((3 * LX * LY * NZ) ** -0.25), 2.5, ((0, 8), (3, 64)), (3, 0, 64, 4.0))
    gauge_links = centred(streams_of[1], (NDISP, 3, 3, 2, NZ, LY * LX), 0.408, 6.0, ((4, 64),), jnp.float32)
    momenta = plant(jax.random.randint(streams_of[2], (NMOM, 3), -2, 3), jax.random.fold_in(streams_of[2], 1), -2, 2).astype(jnp.int32)
    return {"eigenvectors": eigenvectors, "gauge_links": gauge_links, "momenta": momenta}


def plane_phases(momenta, heights, extent):
    site_index = jnp.arange(LX * LY, dtype=jnp.int32)
    across_index = site_index % LX
    along_index = site_index // LX
    x_frac = jnp.mod(momenta[:, 0:1] * across_index[None, :], LX).astype(jnp.float32) / LX
    y_frac = jnp.mod(momenta[:, 1:2] * along_index[None, :], LY).astype(jnp.float32) / LY
    z_frac = jnp.mod(momenta[:, 2:3] * heights[None, :], extent).astype(jnp.float32) / extent
    angles = 2.0 * math.pi * (x_frac[:, None, :] + y_frac[:, None, :] + z_frac[:, :, None])
    return jnp.cos(angles), jnp.sin(angles)


def left_operand(vectors, link, cosines, sines):
    real_vec = vectors[:, :, 0]
    imag_vec = vectors[:, :, 1]
    real_link = link[:, :, 0]
    imag_link = link[:, :, 1]
    real_base = jnp.sum(real_vec[:, :, None] * real_link[None] + imag_vec[:, :, None] * imag_link[None], axis=1)
    imag_base = jnp.sum(real_vec[:, :, None] * imag_link[None] - imag_vec[:, :, None] * real_link[None], axis=1)
    real_left = real_base[None] * cosines[:, None, None] + imag_base[None] * sines[:, None, None]
    imag_left = imag_base[None] * cosines[:, None, None] - real_base[None] * sines[:, None, None]
    return jnp.stack([real_left, imag_left], axis=3).astype(jnp.bfloat16)


def expand(left):
    real_part = left[:, :, :, 0]
    imag_part = left[:, :, :, 1]
    return jnp.stack([jnp.stack([real_part, -imag_part], axis=3), jnp.stack([imag_part, real_part], axis=3)], axis=1)


def roll_across(field):
    shaped = field.reshape(field.shape[:-1] + (LY, LX))
    return jnp.roll(shaped, -1, axis=-1).reshape(field.shape)


def roll_along(field):
    shaped = field.reshape(field.shape[:-1] + (LY, LX))
    return jnp.roll(shaped, -1, axis=-2).reshape(field.shape)


def reference(eigenvectors, gauge_links, momenta):
    extent = eigenvectors.shape[3]

    def advance(running, plane_index):
        current = lax.dynamic_slice_in_dim(eigenvectors, plane_index, 1, 3).astype(jnp.float32)
        upper_index = jnp.mod(plane_index + 1, extent).astype(jnp.int32)
        raised = lax.dynamic_slice_in_dim(eigenvectors, upper_index, 1, 3).astype(jnp.float32)
        link_here = lax.dynamic_slice_in_dim(gauge_links, plane_index, 1, 4)
        cosines, sines = plane_phases(momenta, plane_index[None], extent)
        partners = (roll_across(current), roll_along(current), raised)
        results = []
        for direction in range(NDISP):
            left = expand(left_operand(current, link_here[direction], cosines, sines))
            left = lax.optimization_barrier(left).astype(jnp.float32)
            results.append(jnp.einsum("mqncrzs,jcrzs->mqnj", left, partners[direction], precision=lax.Precision.HIGHEST))
        return running + jnp.stack(results), None

    start_value = jnp.zeros((NDISP, NMOM, 2, NEV, NEV), jnp.float32)
    elementals, _ = lax.scan(advance, start_value, jnp.arange(extent, dtype=jnp.int32))
    return elementals
```

```python
import functools
import math

import jax
import jax.numpy as jnp
from jax import lax
from jax.experimental import pallas as pl
from jax.experimental.pallas import tpu as pltpu
from jax.sharding import PartitionSpec as P

LX = 64
LY = 8
SITES = LX * LY
ROWS = 32
DEPTH = 6 * SITES
VMEM_BYTES = 40 * 1024 * 1024


def moved_across(field):
    lane = lax.broadcasted_iota(jnp.int32, field.shape, 1)
    return jnp.where(
        lane % LX == 0, pltpu.roll(field, SITES - LX + 1, 1), pltpu.roll(field, 1, 1)
    )


def moved_along(field):
    return pltpu.roll(field, LX, 1)


MOVES = (moved_across, moved_along, lambda field: field)


def left_kernel(momenta_ref, height_ref, block_ref, link_ref, left_ref, table_ref):
    row = lax.broadcasted_iota(jnp.int32, (8, SITES), 0) % 4
    site = lax.broadcasted_iota(jnp.int32, (8, SITES), 1)

    def component(k):
        value = jnp.full((8, SITES), momenta_ref[3, k], jnp.int32)
        for p in range(3):
            value = jnp.where(row == p, momenta_ref[p, k], value)
        return value

    x_frac = ((component(0) * (site % LX)) & (LX - 1)).astype(jnp.float32) / LX
    y_frac = ((component(1) * (site // LX)) & (LY - 1)).astype(jnp.float32) / LY
    extent = height_ref[1]
    z_frac = ((component(2) * height_ref[0]) & (extent - 1)).astype(jnp.float32)
    z_frac = z_frac / extent.astype(jnp.float32)
    angles = 2.0 * math.pi * (x_frac + y_frac + z_frac)
    first = lax.broadcasted_iota(jnp.int32, (8, SITES), 0) < 4
    table = jnp.where(first, jnp.cos(angles), jnp.sin(angles))
    for d in range(3):
        table_ref[d] = MOVES[d](table)

    def rows_of(group, carry):
        rows = pl.ds(pl.multiple_of(group * 16, 16), 16)
        for d in range(3):
            for out_colour in range(3):
                real_base = jnp.zeros((16, SITES), jnp.float32)
                imag_base = jnp.zeros((16, SITES), jnp.float32)
                for colour in range(3):
                    at = 2 * SITES * colour
                    real_vec = block_ref[rows, at : at + SITES].astype(jnp.float32)
                    imag_vec = block_ref[rows, at + SITES : at + 2 * SITES].astype(jnp.float32)
                    real_link = link_ref[d, colour, out_colour, 0:1, :]
                    imag_link = link_ref[d, colour, out_colour, 1:2, :]
                    real_base += real_vec * real_link + imag_vec * imag_link
                    imag_base += real_vec * imag_link - imag_vec * real_link
                real_base, imag_base = MOVES[d](real_base), MOVES[d](imag_base)
                at = 2 * SITES * out_colour
                for p in range(4):
                    cosine = table_ref[d, p : p + 1, :]
                    sine = table_ref[d, p + 4 : p + 5, :]
                    left_ref[4 * d + p, rows, at : at + SITES] = (
                        real_base * cosine + imag_base * sine
                    ).astype(jnp.bfloat16)
                    left_ref[4 * d + p, rows, at + SITES : at + 2 * SITES] = (
                        imag_base * cosine - real_base * sine
                    ).astype(jnp.bfloat16)
        return carry

    lax.fori_loop(0, ROWS // 16, rows_of, 0)


def left_operand(momenta, height, block, links):
    return pl.pallas_call(
        left_kernel,
        out_shape=jax.ShapeDtypeStruct((12, ROWS, DEPTH), jnp.bfloat16),
        in_specs=[
            pl.BlockSpec(memory_space=pltpu.SMEM),
            pl.BlockSpec(memory_space=pltpu.SMEM),
            pl.BlockSpec(memory_space=pltpu.VMEM),
            pl.BlockSpec(memory_space=pltpu.VMEM),
        ],
        out_specs=pl.BlockSpec(memory_space=pltpu.VMEM),
        scratch_shapes=[pltpu.VMEM((3, 8, SITES), jnp.float32)],
        compiler_params=pltpu.CompilerParams(vmem_limit_bytes=VMEM_BYTES),
    )(momenta, height, block, links)


def product_kernel(half_ref, own_ref, other_ref, right_ref, raised_ref, out_ref, both_ref):
    def spread(source_ref):
        for colour in range(3):
            at = 2 * SITES * colour
            real_vec = source_ref[:, at : at + SITES]
            imag_vec = source_ref[:, at + SITES : at + 2 * SITES]
            both_ref[0:128, at : at + SITES] = real_vec
            both_ref[0:128, at + SITES : at + 2 * SITES] = -imag_vec
            both_ref[128:256, at : at + SITES] = imag_vec
            both_ref[128:256, at + SITES : at + 2 * SITES] = real_vec

    def multiply(left_ref, half, least, most):
        product = lax.dot_general(
            both_ref[...],
            left_ref[least:most, :],
            (((1,), (1,)), ((), ())),
            preferred_element_type=jnp.float32,
        )
        width = most - least
        real_part = product[0:128].reshape(16, 8, width)
        imag_part = product[128:256].reshape(16, 8, width)
        upper = lax.broadcasted_iota(jnp.int32, (16, 8, width), 1) < 4
        even = jnp.where(upper, real_part, pltpu.roll(imag_part, 4, 1)).astype(jnp.bfloat16)
        odd = jnp.where(upper, pltpu.roll(real_part, 4, 1), imag_part).astype(jnp.bfloat16)
        for block in range(4):
            for pair in range(4):
                out_ref[block, half, 2 * pair, :, least:most] = even[4 * block + pair]
                out_ref[block, half, 2 * pair + 1, :, least:most] = odd[4 * block + pair]

    half = half_ref[0]
    spread(right_ref)
    multiply(own_ref, half, 0, 256)
    multiply(other_ref, 1 - half, 0, 256)
    spread(raised_ref)
    multiply(own_ref, half, 256, 384)
    multiply(other_ref, 1 - half, 256, 384)


def products(half, own, other, right, raised):
    return pl.pallas_call(
        product_kernel,
        out_shape=jax.ShapeDtypeStruct((4, 2, 8, 8, 12 * ROWS), jnp.bfloat16),
        in_specs=[pl.BlockSpec(memory_space=pltpu.SMEM)]
        + [pl.BlockSpec(memory_space=pltpu.VMEM)] * 4,
        out_specs=pl.BlockSpec(memory_space=pltpu.VMEM),
        scratch_shapes=[pltpu.VMEM((256, DEPTH), jnp.bfloat16)],
        compiler_params=pltpu.CompilerParams(vmem_limit_bytes=VMEM_BYTES),
    )(half, own, other, right, raised)


def body(eigenvectors, gauge_links, momenta):
    space = lax.axis_size("space")
    eig = lax.axis_size("eig")
    s = lax.axis_index("space")
    zh = lax.axis_index("eig") % 2
    block = eigenvectors.reshape(ROWS, DEPTH)
    links = gauge_links.reshape(3, 3, 3, 2, SITES)
    height = jnp.stack([s, jnp.int32(space)]).astype(jnp.int32)
    half = zh.astype(jnp.int32).reshape(1)

    partner = lax.ppermute(block, "eig", [(a, a ^ 1) for a in range(eig)])
    right = lax.all_to_all(
        jnp.broadcast_to(block[None], (eig // 2, ROWS, DEPTH)),
        "eig",
        split_axis=0,
        concat_axis=0,
        axis_index_groups=[list(range(0, eig, 2)), list(range(1, eig, 2))],
        tiled=True,
    ).reshape(eig // 2 * ROWS, DEPTH)
    raised = lax.ppermute(right, "space", [((a + 1) % space, a) for a in range(space)])

    own = left_operand(momenta, height, block, links).reshape(12 * ROWS, DEPTH)
    other = left_operand(momenta, height, partner, links).reshape(12 * ROWS, DEPTH)
    chunks = products(half, own, other, right, raised).reshape(space, 8, 12 * ROWS)
    got = lax.all_to_all(chunks, "space", split_axis=0, concat_axis=0, tiled=True)
    total = jnp.sum(got.astype(jnp.float32), axis=0)

    pairs = []
    for a in range(space):
        for b in range(eig):
            if (a // 8) % 2 != b % 2:
                pairs.append((a * eig + b, (a ^ 8) * eig + (b ^ 1)))
    swapped = lax.ppermute(total, ("space", "eig"), pairs)
    final = jnp.where((s // 8) % 2 == zh, total, swapped)
    return final.reshape(2, 4, 3, 4, ROWS).transpose(2, 3, 0, 4, 1)


def solution(mesh):
    return jax.shard_map(
        body,
        mesh=mesh,
        in_specs=(
            P("eig", None, None, "space", None),
            P(None, None, None, None, "space", None),
            P(),
        ),
        out_specs=P(None, None, None, "eig", "space"),
        check_vma=False,
    )
```

```python
import functools
import math

import jax
import jax.numpy as jnp
from jax import lax
from jax.experimental import pallas as pl
from jax.experimental.pallas import tpu as pltpu
from jax.sharding import PartitionSpec as P

LX = 64
LY = 8
SITES = LX * LY
ROWS = 32
DEPTH = 6 * SITES
VMEM_BYTES = 40 * 1024 * 1024


def moved_across(field):
    lane = lax.broadcasted_iota(jnp.int32, field.shape, 1)
    return jnp.where(
        lane % LX == 0, pltpu.roll(field, SITES - LX + 1, 1), pltpu.roll(field, 1, 1)
    )


def moved_along(field):
    return pltpu.roll(field, LX, 1)


MOVES = (moved_across, moved_along, lambda field: field)


def left_kernel(momenta_ref, height_ref, block_ref, link_ref, left_ref, table_ref):
    row = lax.broadcasted_iota(jnp.int32, (8, SITES), 0) % 4
    site = lax.broadcasted_iota(jnp.int32, (8, SITES), 1)

    def component(k):
        value = jnp.full((8, SITES), momenta_ref[3, k], jnp.int32)
        for p in range(3):
            value = jnp.where(row == p, momenta_ref[p, k], value)
        return value

    x_frac = ((component(0) * (site % LX)) & (LX - 1)).astype(jnp.float32) / LX
    y_frac = ((component(1) * (site // LX)) & (LY - 1)).astype(jnp.float32) / LY
    extent = height_ref[1]
    z_frac = ((component(2) * height_ref[0]) & (extent - 1)).astype(jnp.float32)
    z_frac = z_frac / extent.astype(jnp.float32)
    angles = 2.0 * math.pi * (x_frac + y_frac + z_frac)
    first = lax.broadcasted_iota(jnp.int32, (8, SITES), 0) < 4
    table = jnp.where(first, jnp.cos(angles), jnp.sin(angles))
    for d in range(3):
        table_ref[d] = MOVES[d](table)

    def rows_of(group, carry):
        rows = pl.ds(pl.multiple_of(group * 16, 16), 16)
        for d in range(3):
            for out_colour in range(3):
                real_base = jnp.zeros((16, SITES), jnp.float32)
                imag_base = jnp.zeros((16, SITES), jnp.float32)
                for colour in range(3):
                    at = 2 * SITES * colour
                    real_vec = block_ref[rows, at : at + SITES].astype(jnp.float32)
                    imag_vec = block_ref[rows, at + SITES : at + 2 * SITES].astype(jnp.float32)
                    real_link = link_ref[d, colour, out_colour, 0:1, :]
                    imag_link = link_ref[d, colour, out_colour, 1:2, :]
                    real_base += real_vec * real_link + imag_vec * imag_link
                    imag_base += real_vec * imag_link - imag_vec * real_link
                real_base, imag_base = MOVES[d](real_base), MOVES[d](imag_base)
                at = 2 * SITES * out_colour
                for p in range(4):
                    cosine = table_ref[d, p : p + 1, :]
                    sine = table_ref[d, p + 4 : p + 5, :]
                    left_ref[4 * d + p, rows, at : at + SITES] = (
                        real_base * cosine + imag_base * sine
                    ).astype(jnp.bfloat16)
                    left_ref[4 * d + p, rows, at + SITES : at + 2 * SITES] = (
                        imag_base * cosine - real_base * sine
                    ).astype(jnp.bfloat16)
        return carry

    lax.fori_loop(0, ROWS // 16, rows_of, 0)


def left_operand(momenta, height, block, links):
    return pl.pallas_call(
        left_kernel,
        out_shape=jax.ShapeDtypeStruct((12, ROWS, DEPTH), jnp.bfloat16),
        in_specs=[
            pl.BlockSpec(memory_space=pltpu.SMEM),
            pl.BlockSpec(memory_space=pltpu.SMEM),
            pl.BlockSpec(memory_space=pltpu.VMEM),
            pl.BlockSpec(memory_space=pltpu.VMEM),
        ],
        out_specs=pl.BlockSpec(memory_space=pltpu.VMEM),
        scratch_shapes=[pltpu.VMEM((3, 8, SITES), jnp.float32)],
        compiler_params=pltpu.CompilerParams(vmem_limit_bytes=VMEM_BYTES),
    )(momenta, height, block, links)


def product_kernel(half_ref, own_ref, other_ref, right_ref, raised_ref, out_ref, both_ref):
    def spread(source_ref):
        for colour in range(3):
            at = 2 * SITES * colour
            real_vec = source_ref[:, at : at + SITES]
            imag_vec = source_ref[:, at + SITES : at + 2 * SITES]
            both_ref[0:128, at : at + SITES] = real_vec
            both_ref[0:128, at + SITES : at + 2 * SITES] = -imag_vec
            both_ref[128:256, at : at + SITES] = imag_vec
            both_ref[128:256, at + SITES : at + 2 * SITES] = real_vec

    def multiply(left_ref, half, least, most):
        product = lax.dot_general(
            both_ref[...],
            left_ref[least:most, :],
            (((1,), (1,)), ((), ())),
            preferred_element_type=jnp.float32,
        )
        width = most - least
        real_part = product[0:128].reshape(16, 8, width)
        imag_part = product[128:256].reshape(16, 8, width)
        upper = lax.broadcasted_iota(jnp.int32, (16, 8, width), 1) < 4
        even = jnp.where(upper, real_part, pltpu.roll(imag_part, 4, 1)).astype(jnp.bfloat16)
        odd = jnp.where(upper, pltpu.roll(real_part, 4, 1), imag_part).astype(jnp.bfloat16)
        for block in range(4):
            for pair in range(4):
                out_ref[block, half, 2 * pair, :, least:most] = even[4 * block + pair]
                out_ref[block, half, 2 * pair + 1, :, least:most] = odd[4 * block + pair]

    half = half_ref[0]
    spread(right_ref)
    multiply(own_ref, half, 0, 256)
    multiply(other_ref, 1 - half, 0, 256)
    spread(raised_ref)
    multiply(own_ref, half, 256, 384)
    multiply(other_ref, 1 - half, 256, 384)


def products(half, own, other, right, raised):
    return pl.pallas_call(
        product_kernel,
        out_shape=jax.ShapeDtypeStruct((4, 2, 8, 8, 12 * ROWS), jnp.bfloat16),
        in_specs=[pl.BlockSpec(memory_space=pltpu.SMEM)]
        + [pl.BlockSpec(memory_space=pltpu.VMEM)] * 4,
        out_specs=pl.BlockSpec(memory_space=pltpu.VMEM),
        scratch_shapes=[pltpu.VMEM((256, DEPTH), jnp.bfloat16)],
        compiler_params=pltpu.CompilerParams(vmem_limit_bytes=VMEM_BYTES),
    )(half, own, other, right, raised)


def body(eigenvectors, gauge_links, momenta):
    space = lax.axis_size("space")
    eig = lax.axis_size("eig")
    s = lax.axis_index("space")
    zh = lax.axis_index("eig") % 2
    block = eigenvectors.reshape(ROWS, DEPTH)
    links = gauge_links.reshape(3, 3, 3, 2, SITES)
    height = jnp.stack([s, jnp.int32(space)]).astype(jnp.int32)
    half = zh.astype(jnp.int32).reshape(1)

    partner = lax.ppermute(block, "eig", [(a, a ^ 1) for a in range(eig)])
    right = lax.all_gather(
        block,
        "eig",
        axis_index_groups=[list(range(0, eig, 2)), list(range(1, eig, 2))],
        tiled=True,
    )
    right, partner = lax.optimization_barrier((right, partner))
    raised = lax.ppermute(right, "space", [((a + 1) % space, a) for a in range(space)])

    own = left_operand(momenta, height, block, links).reshape(12 * ROWS, DEPTH)
    other = left_operand(momenta, height, partner, links).reshape(12 * ROWS, DEPTH)
    chunks = products(half, own, other, right, raised).reshape(space, 8, 12 * ROWS)
    got = lax.all_to_all(chunks, "space", split_axis=0, concat_axis=0, tiled=True)
    total = jnp.sum(got.astype(jnp.float32), axis=0)

    pairs = []
    for a in range(space):
        for b in range(eig):
            if (a // 8) % 2 != b % 2:
                pairs.append((a * eig + b, (a ^ 8) * eig + (b ^ 1)))
    swapped = lax.ppermute(total, ("space", "eig"), pairs)
    final = jnp.where((s // 8) % 2 == zh, total, swapped)
    return final.reshape(2, 4, 3, 4, ROWS).transpose(2, 3, 0, 4, 1)


def solution(mesh):
    return jax.shard_map(
        body,
        mesh=mesh,
        in_specs=(
            P("eig", None, None, "space", None),
            P(None, None, None, None, "space", None),
            P(),
        ),
        out_specs=P(None, None, None, "eig", "space"),
        check_vma=False,
    )
```

```python
import functools
import math

import jax
import jax.numpy as jnp
from jax import lax
from jax.experimental import pallas as pl
from jax.experimental.pallas import tpu as pltpu
from jax.sharding import PartitionSpec as P

LX = 64
LY = 8
SITES = LX * LY
ROWS = 32
DEPTH = 6 * SITES
VMEM_BYTES = 40 * 1024 * 1024


def moved_across(field):
    lane = lax.broadcasted_iota(jnp.int32, field.shape, 1)
    return jnp.where(
        lane % LX == 0, pltpu.roll(field, SITES - LX + 1, 1), pltpu.roll(field, 1, 1)
    )


def moved_along(field):
    return pltpu.roll(field, LX, 1)


MOVES = (moved_across, moved_along, lambda field: field)


def left_kernel(momenta_ref, height_ref, block_ref, link_ref, left_ref, table_ref):
    row = lax.broadcasted_iota(jnp.int32, (8, SITES), 0) % 4
    site = lax.broadcasted_iota(jnp.int32, (8, SITES), 1)

    def component(k):
        value = jnp.full((8, SITES), momenta_ref[3, k], jnp.int32)
        for p in range(3):
            value = jnp.where(row == p, momenta_ref[p, k], value)
        return value

    x_frac = ((component(0) * (site % LX)) & (LX - 1)).astype(jnp.float32) / LX
    y_frac = ((component(1) * (site // LX)) & (LY - 1)).astype(jnp.float32) / LY
    extent = height_ref[1]
    z_frac = ((component(2) * height_ref[0]) & (extent - 1)).astype(jnp.float32)
    z_frac = z_frac / extent.astype(jnp.float32)
    angles = 2.0 * math.pi * (x_frac + y_frac + z_frac)
    first = lax.broadcasted_iota(jnp.int32, (8, SITES), 0) < 4
    table = jnp.where(first, jnp.cos(angles), jnp.sin(angles))
    for d in range(3):
        table_ref[d] = MOVES[d](table)

    def rows_of(group, carry):
        rows = pl.ds(pl.multiple_of(group * 16, 16), 16)
        for d in range(3):
            for out_colour in range(3):
                real_base = jnp.zeros((16, SITES), jnp.float32)
                imag_base = jnp.zeros((16, SITES), jnp.float32)
                for colour in range(3):
                    at = 2 * SITES * colour
                    real_vec = block_ref[rows, at : at + SITES].astype(jnp.float32)
                    imag_vec = block_ref[rows, at + SITES : at + 2 * SITES].astype(jnp.float32)
                    real_link = link_ref[d, colour, out_colour, 0:1, :]
                    imag_link = link_ref[d, colour, out_colour, 1:2, :]
                    real_base += real_vec * real_link + imag_vec * imag_link
                    imag_base += real_vec * imag_link - imag_vec * real_link
                real_base, imag_base = MOVES[d](real_base), MOVES[d](imag_base)
                at = 2 * SITES * out_colour
                for p in range(4):
                    cosine = table_ref[d, p : p + 1, :]
                    sine = table_ref[d, p + 4 : p + 5, :]
                    left_ref[4 * d + p, rows, at : at + SITES] = (
                        real_base * cosine + imag_base * sine
                    ).astype(jnp.bfloat16)
                    left_ref[4 * d + p, rows, at + SITES : at + 2 * SITES] = (
                        imag_base * cosine - real_base * sine
                    ).astype(jnp.bfloat16)
        return carry

    lax.fori_loop(0, ROWS // 16, rows_of, 0)


def left_operand(momenta, height, block, links):
    return pl.pallas_call(
        left_kernel,
        out_shape=jax.ShapeDtypeStruct((12, ROWS, DEPTH), jnp.bfloat16),
        in_specs=[
            pl.BlockSpec(memory_space=pltpu.SMEM),
            pl.BlockSpec(memory_space=pltpu.SMEM),
            pl.BlockSpec(memory_space=pltpu.VMEM),
            pl.BlockSpec(memory_space=pltpu.VMEM),
        ],
        out_specs=pl.BlockSpec(memory_space=pltpu.VMEM),
        scratch_shapes=[pltpu.VMEM((3, 8, SITES), jnp.float32)],
        compiler_params=pltpu.CompilerParams(vmem_limit_bytes=VMEM_BYTES),
    )(momenta, height, block, links)


def product_kernel(half_ref, own_ref, other_ref, right_ref, raised_ref, out_ref, both_ref):
    def spread(source_ref):
        for colour in range(3):
            at = 2 * SITES * colour
            real_vec = source_ref[:, at : at + SITES]
            imag_vec = source_ref[:, at + SITES : at + 2 * SITES]
            both_ref[0:128, at : at + SITES] = real_vec
            both_ref[0:128, at + SITES : at + 2 * SITES] = -imag_vec
            both_ref[128:256, at : at + SITES] = imag_vec
            both_ref[128:256, at + SITES : at + 2 * SITES] = real_vec

    def multiply(left_ref, half, least, most):
        product = lax.dot_general(
            both_ref[...],
            left_ref[least:most, :],
            (((1,), (1,)), ((), ())),
            preferred_element_type=jnp.float32,
        )
        width = most - least
        real_part = product[0:128].reshape(16, 8, width)
        imag_part = product[128:256].reshape(16, 8, width)
        upper = lax.broadcasted_iota(jnp.int32, (16, 8, width), 1) < 4
        even = jnp.where(upper, real_part, pltpu.roll(imag_part, 4, 1)).astype(jnp.bfloat16)
        odd = jnp.where(upper, pltpu.roll(real_part, 4, 1), imag_part).astype(jnp.bfloat16)
        for block in range(4):
            for pair in range(4):
                out_ref[2 * pair, block, half, :, least:most] = even[4 * block + pair]
                out_ref[2 * pair + 1, block, half, :, least:most] = odd[4 * block + pair]

    half = half_ref[0]
    spread(right_ref)
    multiply(own_ref, half, 0, 256)
    multiply(other_ref, 1 - half, 0, 256)
    spread(raised_ref)
    multiply(own_ref, half, 256, 384)
    multiply(other_ref, 1 - half, 256, 384)


def products(half, own, other, right, raised):
    return pl.pallas_call(
        product_kernel,
        out_shape=jax.ShapeDtypeStruct((8, 4, 2, 8, 12 * ROWS), jnp.bfloat16),
        in_specs=[pl.BlockSpec(memory_space=pltpu.SMEM)]
        + [pl.BlockSpec(memory_space=pltpu.VMEM)] * 4,
        out_specs=pl.BlockSpec(memory_space=pltpu.VMEM),
        scratch_shapes=[pltpu.VMEM((256, DEPTH), jnp.bfloat16)],
        compiler_params=pltpu.CompilerParams(vmem_limit_bytes=VMEM_BYTES),
    )(half, own, other, right, raised)


def body(eigenvectors, gauge_links, momenta):
    space = lax.axis_size("space")
    eig = lax.axis_size("eig")
    s = lax.axis_index("space")
    zh = lax.axis_index("eig") % 2
    block = eigenvectors.reshape(ROWS, DEPTH)
    links = gauge_links.reshape(3, 3, 3, 2, SITES)
    height = jnp.stack([s, jnp.int32(space)]).astype(jnp.int32)
    half = zh.astype(jnp.int32).reshape(1)

    partner = lax.ppermute(block, "eig", [(a, a ^ 1) for a in range(eig)])
    right = lax.all_gather(
        block,
        "eig",
        axis_index_groups=[list(range(0, eig, 2)), list(range(1, eig, 2))],
        tiled=True,
    )
    right, partner = lax.optimization_barrier((right, partner))
    raised = lax.ppermute(right, "space", [((a + 1) % space, a) for a in range(space)])

    own = left_operand(momenta, height, block, links).reshape(12 * ROWS, DEPTH)
    other = left_operand(momenta, height, partner, links).reshape(12 * ROWS, DEPTH)
    chunks = products(half, own, other, right, raised)
    near = [list(range(start, start + 8)) for start in range(0, space, 8)]
    far = [list(range(start, space, 8)) for start in range(8)]
    chunks = chunks.reshape(8, 64, 12 * ROWS)
    got = lax.all_to_all(
        chunks, "space", split_axis=0, concat_axis=0, axis_index_groups=near, tiled=True
    )
    sums = jnp.sum(got.astype(jnp.float32), axis=0).reshape(space // 8, 8, 12 * ROWS)
    got = lax.all_to_all(
        sums, "space", split_axis=0, concat_axis=0, axis_index_groups=far, tiled=True
    )
    total = jnp.sum(got, axis=0)

    pairs = []
    for a in range(space):
        for b in range(eig):
            if (a // 8) % 2 != b % 2:
                pairs.append((a * eig + b, (a ^ 8) * eig + (b ^ 1)))
    swapped = lax.ppermute(total, ("space", "eig"), pairs)
    final = jnp.where((s // 8) % 2 == zh, total, swapped)
    return final.reshape(2, 4, 3, 4, ROWS).transpose(2, 3, 0, 4, 1)


def solution(mesh):
    return jax.shard_map(
        body,
        mesh=mesh,
        in_specs=(
            P("eig", None, None, "space", None),
            P(None, None, None, None, "space", None),
            P(),
        ),
        out_specs=P(None, None, None, "eig", "space"),
        check_vma=False,
    )
```

```python
import math

import jax
import jax.numpy as jnp
from jax import lax
from jax.experimental import pallas as pl
from jax.experimental.pallas import tpu as pltpu
from jax.sharding import PartitionSpec as P

LX = 64
LY = 8
SITES = LX * LY
ROWS = 32
DEPTH = 6 * SITES
VMEM_BYTES = 40 * 1024 * 1024


def moved_across(field):
    lane = lax.broadcasted_iota(jnp.int32, field.shape, 1)
    return jnp.where(
        lane % LX == 0, pltpu.roll(field, SITES - LX + 1, 1), pltpu.roll(field, 1, 1)
    )


def moved_along(field):
    return pltpu.roll(field, LX, 1)


MOVES = (moved_across, moved_along, lambda field: field)


def left_kernel(momenta_ref, height_ref, block_ref, below_ref, link_ref, link_below_ref, left_ref, table_ref):
    row = lax.broadcasted_iota(jnp.int32, (8, SITES), 0) % 4
    site = lax.broadcasted_iota(jnp.int32, (8, SITES), 1)

    def component(k):
        value = jnp.full((8, SITES), momenta_ref[3, k], jnp.int32)
        for p in range(3):
            value = jnp.where(row == p, momenta_ref[p, k], value)
        return value

    x_frac = ((component(0) * (site % LX)) & (LX - 1)).astype(jnp.float32) / LX
    y_frac = ((component(1) * (site // LX)) & (LY - 1)).astype(jnp.float32) / LY
    extent = height_ref[1]
    first = lax.broadcasted_iota(jnp.int32, (8, SITES), 0) < 4

    def plane_table(height):
        z_frac = ((component(2) * height) & (extent - 1)).astype(jnp.float32)
        z_frac = z_frac / extent.astype(jnp.float32)
        angles = 2.0 * math.pi * (x_frac + y_frac + z_frac)
        return jnp.where(first, jnp.cos(angles), jnp.sin(angles))

    here = plane_table(height_ref[0])
    table_ref[0] = moved_across(here)
    table_ref[1] = moved_along(here)
    table_ref[2] = plane_table((height_ref[0] - 1) & (extent - 1))

    def rows_of(group, carry):
        rows = pl.ds(pl.multiple_of(group * 16, 16), 16)
        for d in range(3):
            source_ref = below_ref if d == 2 else block_ref
            for out_colour in range(3):
                real_base = jnp.zeros((16, SITES), jnp.float32)
                imag_base = jnp.zeros((16, SITES), jnp.float32)
                for colour in range(3):
                    at = 2 * SITES * colour
                    real_vec = source_ref[rows, at : at + SITES].astype(jnp.float32)
                    imag_vec = source_ref[rows, at + SITES : at + 2 * SITES].astype(jnp.float32)
                    if d == 2:
                        real_link = link_below_ref[colour, out_colour, 0:1, :]
                        imag_link = link_below_ref[colour, out_colour, 1:2, :]
                    else:
                        real_link = link_ref[d, colour, out_colour, 0:1, :]
                        imag_link = link_ref[d, colour, out_colour, 1:2, :]
                    real_base += real_vec * real_link + imag_vec * imag_link
                    imag_base += real_vec * imag_link - imag_vec * real_link
                real_base, imag_base = MOVES[d](real_base), MOVES[d](imag_base)
                at = 2 * SITES * out_colour
                for p in range(4):
                    cosine = table_ref[d, p : p + 1, :]
                    sine = table_ref[d, p + 4 : p + 5, :]
                    left_ref[4 * d + p, rows, at : at + SITES] = (
                        real_base * cosine + imag_base * sine
                    ).astype(jnp.bfloat16)
                    left_ref[4 * d + p, rows, at + SITES : at + 2 * SITES] = (
                        imag_base * cosine - real_base * sine
                    ).astype(jnp.bfloat16)
        return carry

    lax.fori_loop(0, ROWS // 16, rows_of, 0)


def left_operand(momenta, height, block, below, links, link_below):
    return pl.pallas_call(
        left_kernel,
        out_shape=jax.ShapeDtypeStruct((12, ROWS, DEPTH), jnp.bfloat16),
        in_specs=[pl.BlockSpec(memory_space=pltpu.SMEM)] * 2
        + [pl.BlockSpec(memory_space=pltpu.VMEM)] * 4,
        out_specs=pl.BlockSpec(memory_space=pltpu.VMEM),
        scratch_shapes=[pltpu.VMEM((3, 8, SITES), jnp.float32)],
        compiler_params=pltpu.CompilerParams(vmem_limit_bytes=VMEM_BYTES),
    )(momenta, height, block, below, links, link_below)


def product_kernel(half_ref, left_ref, near_ref, far_ref, out_ref, both_ref):
    def spread(source_ref):
        for colour in range(3):
            at = 2 * SITES * colour
            real_vec = source_ref[:, at : at + SITES]
            imag_vec = source_ref[:, at + SITES : at + 2 * SITES]
            both_ref[0:128, at : at + SITES] = real_vec
            both_ref[0:128, at + SITES : at + 2 * SITES] = -imag_vec
            both_ref[128:256, at : at + SITES] = imag_vec
            both_ref[128:256, at + SITES : at + 2 * SITES] = real_vec

    def multiply(half):
        product = lax.dot_general(
            both_ref[...],
            left_ref[...],
            (((1,), (1,)), ((), ())),
            preferred_element_type=jnp.float32,
        )
        width = 12 * ROWS
        real_part = product[0:128].reshape(16, 8, width)
        imag_part = product[128:256].reshape(16, 8, width)
        upper = lax.broadcasted_iota(jnp.int32, (16, 8, width), 1) < 4
        even = jnp.where(upper, real_part, pltpu.roll(imag_part, 4, 1)).astype(jnp.bfloat16)
        odd = jnp.where(upper, pltpu.roll(real_part, 4, 1), imag_part).astype(jnp.bfloat16)
        for block in range(4):
            for pair in range(4):
                out_ref[block, half, 2 * pair] = even[4 * block + pair]
                out_ref[block, half, 2 * pair + 1] = odd[4 * block + pair]

    half = half_ref[0]
    spread(near_ref)
    multiply(half)
    spread(far_ref)
    multiply(1 - half)


def products(half, left, near, far):
    return pl.pallas_call(
        product_kernel,
        out_shape=jax.ShapeDtypeStruct((4, 2, 8, 8, 12 * ROWS), jnp.bfloat16),
        in_specs=[pl.BlockSpec(memory_space=pltpu.SMEM)]
        + [pl.BlockSpec(memory_space=pltpu.VMEM)] * 3,
        out_specs=pl.BlockSpec(memory_space=pltpu.VMEM),
        scratch_shapes=[pltpu.VMEM((256, DEPTH), jnp.bfloat16)],
        compiler_params=pltpu.CompilerParams(vmem_limit_bytes=VMEM_BYTES),
    )(half, left, near, far)


def body(eigenvectors, gauge_links, momenta):
    space = lax.axis_size("space")
    eig = lax.axis_size("eig")
    s = lax.axis_index("space")
    e = lax.axis_index("eig")
    block = eigenvectors.reshape(ROWS, DEPTH)
    links = gauge_links.reshape(3, 3, 3, 2, SITES)
    height = jnp.stack([s, jnp.int32(space)]).astype(jnp.int32)
    half = (e & 1).astype(jnp.int32).reshape(1)

    def from_below(value):
        return lax.ppermute(value, "space", [(a, (a + 1) % space) for a in range(space)])

    def around_x(value):
        groups = [list(range(0, eig, 2)), list(range(1, eig, 2))]
        return lax.all_gather(value, "eig", axis_index_groups=groups, tiled=True)

    partner = lax.ppermute(block, "eig", [(a, a ^ 1) for a in range(eig)])
    near = around_x(block)
    below = from_below(block)
    link_below = from_below(links[2])
    left = left_operand(momenta, height, block, below, links, link_below)
    left = left.reshape(12 * ROWS, DEPTH)

    partner, left, near = lax.optimization_barrier((partner, left, near))
    far = around_x(partner)
    chunks = products(half, left, near, far).reshape(space, 8, 12 * ROWS)
    got = lax.all_to_all(chunks, "space", split_axis=0, concat_axis=0, tiled=True)
    total = jnp.sum(got.astype(jnp.float32), axis=0)
    return total.reshape(2, 4, 3, 4, ROWS).transpose(2, 3, 0, 4, 1)


def solution(mesh):
    return jax.shard_map(
        body,
        mesh=mesh,
        in_specs=(
            P("eig", None, None, "space", None),
            P(None, None, None, None, "space", None),
            P(),
        ),
        out_specs=P(None, None, None, "eig", "space"),
        check_vma=False,
    )
```

```python
import math

import jax
import jax.numpy as jnp
from jax import lax
from jax.experimental import pallas as pl
from jax.experimental.pallas import tpu as pltpu
from jax.sharding import PartitionSpec as P

LX = 64
LY = 8
SITES = LX * LY
ROWS = 32
DEPTH = 6 * SITES
VMEM_BYTES = 40 * 1024 * 1024


def moved_across(field):
    lane = lax.broadcasted_iota(jnp.int32, field.shape, 1)
    return jnp.where(
        lane % LX == 0, pltpu.roll(field, SITES - LX + 1, 1), pltpu.roll(field, 1, 1)
    )


def moved_along(field):
    return pltpu.roll(field, LX, 1)


MOVES = (moved_across, moved_along, lambda field: field)


def left_kernel(momenta_ref, height_ref, block_ref, below_ref, link_ref, link_below_ref, left_ref, table_ref):
    row = lax.broadcasted_iota(jnp.int32, (8, SITES), 0) % 4
    site = lax.broadcasted_iota(jnp.int32, (8, SITES), 1)

    def component(k):
        value = jnp.full((8, SITES), momenta_ref[3, k], jnp.int32)
        for p in range(3):
            value = jnp.where(row == p, momenta_ref[p, k], value)
        return value

    x_frac = ((component(0) * (site % LX)) & (LX - 1)).astype(jnp.float32) / LX
    y_frac = ((component(1) * (site // LX)) & (LY - 1)).astype(jnp.float32) / LY
    extent = height_ref[1]
    first = lax.broadcasted_iota(jnp.int32, (8, SITES), 0) < 4

    def plane_table(height):
        z_frac = ((component(2) * height) & (extent - 1)).astype(jnp.float32)
        z_frac = z_frac / extent.astype(jnp.float32)
        angles = 2.0 * math.pi * (x_frac + y_frac + z_frac)
        return jnp.where(first, jnp.cos(angles), jnp.sin(angles))

    here = plane_table(height_ref[0])
    table_ref[0] = moved_across(here)
    table_ref[1] = moved_along(here)
    table_ref[2] = plane_table((height_ref[0] - 1) & (extent - 1))

    def rows_of(group, carry):
        rows = pl.ds(pl.multiple_of(group * 16, 16), 16)
        for d in range(3):
            source_ref = below_ref if d == 2 else block_ref
            for out_colour in range(3):
                real_base = jnp.zeros((16, SITES), jnp.float32)
                imag_base = jnp.zeros((16, SITES), jnp.float32)
                for colour in range(3):
                    at = 2 * SITES * colour
                    real_vec = source_ref[rows, at : at + SITES].astype(jnp.float32)
                    imag_vec = source_ref[rows, at + SITES : at + 2 * SITES].astype(jnp.float32)
                    if d == 2:
                        real_link = link_below_ref[2, colour, out_colour, 0]
                        imag_link = link_below_ref[2, colour, out_colour, 1]
                    else:
                        real_link = link_ref[d, colour, out_colour, 0]
                        imag_link = link_ref[d, colour, out_colour, 1]
                    real_base += real_vec * real_link + imag_vec * imag_link
                    imag_base += real_vec * imag_link - imag_vec * real_link
                real_base, imag_base = MOVES[d](real_base), MOVES[d](imag_base)
                at = 2 * SITES * out_colour
                for p in range(4):
                    cosine = table_ref[d, p : p + 1, :]
                    sine = table_ref[d, p + 4 : p + 5, :]
                    left_ref[4 * d + p, rows, at : at + SITES] = (
                        real_base * cosine + imag_base * sine
                    ).astype(jnp.bfloat16)
                    left_ref[4 * d + p, rows, at + SITES : at + 2 * SITES] = (
                        imag_base * cosine - real_base * sine
                    ).astype(jnp.bfloat16)
        return carry

    lax.fori_loop(0, ROWS // 16, rows_of, 0)


def left_operand(momenta, height, block, below, links, link_below):
    return pl.pallas_call(
        left_kernel,
        out_shape=jax.ShapeDtypeStruct((12, ROWS, DEPTH), jnp.bfloat16),
        in_specs=[pl.BlockSpec(memory_space=pltpu.SMEM)] * 2
        + [pl.BlockSpec(memory_space=pltpu.VMEM)] * 4,
        out_specs=pl.BlockSpec(memory_space=pltpu.VMEM),
        scratch_shapes=[pltpu.VMEM((3, 8, SITES), jnp.float32)],
        compiler_params=pltpu.CompilerParams(vmem_limit_bytes=VMEM_BYTES),
    )(momenta, height, block, below, links, link_below)


def product_kernel(where_ref, left_ref, *refs):
    near_refs, (far_ref, out_ref, both_ref) = refs[:4], refs[4:]

    def spread(source_ref, to, rows):
        for colour in range(3):
            at = 2 * SITES * colour
            real_vec = source_ref[:, at : at + SITES]
            imag_vec = source_ref[:, at + SITES : at + 2 * SITES]
            both_ref[to : to + rows, at : at + SITES] = real_vec
            both_ref[to : to + rows, at + SITES : at + 2 * SITES] = -imag_vec
            both_ref[to + 128 : to + 128 + rows, at : at + SITES] = imag_vec
            both_ref[to + 128 : to + 128 + rows, at + SITES : at + 2 * SITES] = real_vec

    def multiply(half, first):
        product = lax.dot_general(
            both_ref[...],
            left_ref[...],
            (((1,), (1,)), ((), ())),
            preferred_element_type=jnp.float32,
        )
        width = 12 * ROWS
        real_part = product[0:128].reshape(16, 8, width)
        imag_part = product[128:256].reshape(16, 8, width)
        upper = lax.broadcasted_iota(jnp.int32, (16, 8, width), 1) < 4
        even = jnp.where(upper, real_part, pltpu.roll(imag_part, 4, 1)).astype(jnp.bfloat16)
        odd = jnp.where(upper, pltpu.roll(real_part, 4, 1), imag_part).astype(jnp.bfloat16)
        for block in range(4):
            to = (first + block) & 3
            for pair in range(4):
                out_ref[to, half, 2 * pair] = even[4 * block + pair]
                out_ref[to, half, 2 * pair + 1] = odd[4 * block + pair]

    half = where_ref[0]
    for block in range(4):
        spread(near_refs[block], ROWS * block, ROWS)
    multiply(half, where_ref[1])
    spread(far_ref, 0, 128)
    multiply(1 - half, 0)


def products(where, left, near, far):
    return pl.pallas_call(
        product_kernel,
        out_shape=jax.ShapeDtypeStruct((4, 2, 8, 8, 12 * ROWS), jnp.bfloat16),
        in_specs=[pl.BlockSpec(memory_space=pltpu.SMEM)]
        + [pl.BlockSpec(memory_space=pltpu.VMEM)] * 6,
        out_specs=pl.BlockSpec(memory_space=pltpu.VMEM),
        scratch_shapes=[pltpu.VMEM((256, DEPTH), jnp.bfloat16)],
        compiler_params=pltpu.CompilerParams(vmem_limit_bytes=VMEM_BYTES),
    )(where, left, *near, far)


def body(eigenvectors, gauge_links, momenta):
    space = lax.axis_size("space")
    eig = lax.axis_size("eig")
    s = lax.axis_index("space")
    e = lax.axis_index("eig")
    block = eigenvectors.reshape(ROWS, DEPTH)
    height = jnp.stack([s, jnp.int32(space)]).astype(jnp.int32)
    where = jnp.stack([e & 1, e >> 1]).astype(jnp.int32)

    def from_below(value):
        return lax.ppermute(value, "space", [(a, (a + 1) % space) for a in range(space)])

    def from_x(value, steps):
        return lax.ppermute(value, "eig", [((a + 2 * steps) % eig, a) for a in range(eig)])

    partner = lax.ppermute(block, "eig", [(a, a ^ 1) for a in range(eig)])
    links_below = from_below(gauge_links)
    later, links_below = lax.optimization_barrier((block, links_below))
    below = from_below(later)
    before, after, opposite = from_x(later, 3), from_x(later, 1), from_x(later, 2)
    left = left_operand(momenta, height, block, below, gauge_links, links_below)
    left = left.reshape(12 * ROWS, DEPTH)

    partner, left = lax.optimization_barrier((partner, left))
    partner, before, after, opposite = lax.optimization_barrier(
        (partner, before, after, opposite)
    )
    groups = [list(range(0, eig, 2)), list(range(1, eig, 2))]
    far = lax.all_gather(partner, "eig", axis_index_groups=groups, tiled=True)
    chunks = products(where, left, (block, after, opposite, before), far).reshape(space, 8, 12 * ROWS)
    got = lax.all_to_all(chunks, "space", split_axis=0, concat_axis=0, tiled=True)
    total = jnp.sum(got.astype(jnp.float32), axis=0)
    return total.reshape(2, 4, 3, 4, ROWS).transpose(2, 3, 0, 4, 1)


def solution(mesh):
    return jax.shard_map(
        body,
        mesh=mesh,
        in_specs=(
            P("eig", None, None, "space", None),
            P(None, None, None, None, "space", None),
            P(),
        ),
        out_specs=P(None, None, None, "eig", "space"),
        check_vma=False,
    )
```

```python
import math

import jax
import jax.numpy as jnp
from jax import lax
from jax.experimental import pallas as pl
from jax.experimental.pallas import tpu as pltpu
from jax.sharding import PartitionSpec as P

LX = 64
LY = 8
SITES = LX * LY
ROWS = 32
DEPTH = 6 * SITES
VMEM_BYTES = 40 * 1024 * 1024


def moved_across(field):
    lane = lax.broadcasted_iota(jnp.int32, field.shape, 1)
    return jnp.where(
        lane % LX == 0, pltpu.roll(field, SITES - LX + 1, 1), pltpu.roll(field, 1, 1)
    )


def moved_along(field):
    return pltpu.roll(field, LX, 1)


MOVES = (moved_across, moved_along, lambda field: field)


def left_kernel(plane_ref, block_ref, link_ref, left_ref, raised_ref, table_ref):
    row = lax.broadcasted_iota(jnp.int32, (8, SITES), 0) % 4
    site = lax.broadcasted_iota(jnp.int32, (8, SITES), 1)

    def component(k):
        value = jnp.full((8, SITES), plane_ref[3, k], jnp.int32)
        for p in range(3):
            value = jnp.where(row == p, plane_ref[p, k], value)
        return value

    x_frac = ((component(0) * (site % LX)) & (LX - 1)).astype(jnp.float32) / LX
    y_frac = ((component(1) * (site // LX)) & (LY - 1)).astype(jnp.float32) / LY
    extent = plane_ref[4, 1]
    z_frac = ((component(2) * plane_ref[4, 0]) & (extent - 1)).astype(jnp.float32)
    z_frac = z_frac / extent.astype(jnp.float32)
    angles = 2.0 * math.pi * (x_frac + y_frac + z_frac)
    first = lax.broadcasted_iota(jnp.int32, (8, SITES), 0) < 4
    table = jnp.where(first, jnp.cos(angles), jnp.sin(angles))
    for d in range(3):
        table_ref[d] = MOVES[d](table)

    def rows_of(group, carry):
        rows = pl.ds(pl.multiple_of(group * 16, 16), 16)
        for d in range(3):
            for out_colour in range(3):
                real_base = jnp.zeros((16, SITES), jnp.float32)
                imag_base = jnp.zeros((16, SITES), jnp.float32)
                for colour in range(3):
                    at = 2 * SITES * colour
                    real_vec = block_ref[rows, at : at + SITES].astype(jnp.float32)
                    imag_vec = block_ref[rows, at + SITES : at + 2 * SITES].astype(jnp.float32)
                    real_link = link_ref[d, colour, out_colour, 0]
                    imag_link = link_ref[d, colour, out_colour, 1]
                    real_base += real_vec * real_link + imag_vec * imag_link
                    imag_base += real_vec * imag_link - imag_vec * real_link
                real_base, imag_base = MOVES[d](real_base), MOVES[d](imag_base)
                at = 2 * SITES * out_colour
                to_ref, to = (raised_ref, 0) if d == 2 else (left_ref, 4 * d)
                for p in range(4):
                    cosine = table_ref[d, p : p + 1, :]
                    sine = table_ref[d, p + 4 : p + 5, :]
                    to_ref[to + p, rows, at : at + SITES] = (
                        real_base * cosine + imag_base * sine
                    ).astype(jnp.bfloat16)
                    to_ref[to + p, rows, at + SITES : at + 2 * SITES] = (
                        imag_base * cosine - real_base * sine
                    ).astype(jnp.bfloat16)
        return carry

    lax.fori_loop(0, ROWS // 16, rows_of, 0)


def left_operand(plane, block, links):
    return pl.pallas_call(
        left_kernel,
        out_shape=[
            jax.ShapeDtypeStruct((8, ROWS, DEPTH), jnp.bfloat16),
            jax.ShapeDtypeStruct((4, ROWS, DEPTH), jnp.bfloat16),
        ],
        in_specs=[pl.BlockSpec(memory_space=pltpu.SMEM)]
        + [pl.BlockSpec(memory_space=pltpu.VMEM)] * 2,
        out_specs=[pl.BlockSpec(memory_space=pltpu.VMEM)] * 2,
        scratch_shapes=[pltpu.VMEM((3, 8, SITES), jnp.float32)],
        compiler_params=pltpu.CompilerParams(vmem_limit_bytes=VMEM_BYTES),
    )(plane, block, links)


def product_kernel(half_ref, left_ref, raised_ref, near_ref, far_ref, out_ref, both_ref):
    def spread(source_ref):
        for colour in range(3):
            at = 2 * SITES * colour
            real_vec = source_ref[:, at : at + SITES]
            imag_vec = source_ref[:, at + SITES : at + 2 * SITES]
            both_ref[0:128, at : at + SITES] = real_vec
            both_ref[0:128, at + SITES : at + 2 * SITES] = -imag_vec
            both_ref[128:256, at : at + SITES] = imag_vec
            both_ref[128:256, at + SITES : at + 2 * SITES] = real_vec

    def multiply(source_ref, half, least, most):
        product = lax.dot_general(
            both_ref[...],
            source_ref[...],
            (((1,), (1,)), ((), ())),
            preferred_element_type=jnp.float32,
        )
        width = most - least
        real_part = product[0:128].reshape(16, 8, width)
        imag_part = product[128:256].reshape(16, 8, width)
        upper = lax.broadcasted_iota(jnp.int32, (16, 8, width), 1) < 4
        even = jnp.where(upper, real_part, pltpu.roll(imag_part, 4, 1)).astype(jnp.bfloat16)
        odd = jnp.where(upper, pltpu.roll(real_part, 4, 1), imag_part).astype(jnp.bfloat16)
        for block in range(4):
            for pair in range(4):
                out_ref[block, half, 2 * pair, :, least:most] = even[4 * block + pair]
                out_ref[block, half, 2 * pair + 1, :, least:most] = odd[4 * block + pair]

    for source_ref, half in ((near_ref, half_ref[0]), (far_ref, 1 - half_ref[0])):
        spread(source_ref)
        multiply(left_ref, half, 0, 8 * ROWS)
        multiply(raised_ref, half, 8 * ROWS, 12 * ROWS)


def products(half, left, raised, near, far):
    return pl.pallas_call(
        product_kernel,
        out_shape=jax.ShapeDtypeStruct((4, 2, 8, 8, 12 * ROWS), jnp.bfloat16),
        in_specs=[pl.BlockSpec(memory_space=pltpu.SMEM)]
        + [pl.BlockSpec(memory_space=pltpu.VMEM)] * 4,
        out_specs=pl.BlockSpec(memory_space=pltpu.VMEM),
        scratch_shapes=[pltpu.VMEM((256, DEPTH), jnp.bfloat16)],
        compiler_params=pltpu.CompilerParams(vmem_limit_bytes=VMEM_BYTES),
    )(half, left, raised, near, far)


def body(eigenvectors, gauge_links, momenta):
    space = lax.axis_size("space")
    eig = lax.axis_size("eig")
    s = lax.axis_index("space")
    e = lax.axis_index("eig")
    block = eigenvectors.reshape(ROWS, DEPTH)
    row = lax.broadcasted_iota(jnp.int32, (5, 3), 0)
    column = lax.broadcasted_iota(jnp.int32, (5, 3), 1)
    plane = jnp.where(column == 0, s, space).astype(jnp.int32)
    plane = jnp.where(row < 4, jnp.pad(momenta, ((0, 1), (0, 0))), plane)
    half = (e & 1).astype(jnp.int32).reshape(1)
    groups = [list(range(0, eig, 2)), list(range(1, eig, 2))]

    def around_x(value):
        return lax.all_gather(value, "eig", axis_index_groups=groups, tiled=True)

    partner = lax.ppermute(block, "eig", [(a, a ^ 1) for a in range(eig)])
    near = around_x(block)
    near, plane = lax.optimization_barrier((near, plane))
    left, raised = left_operand(plane, block, gauge_links)

    partner, near, left, raised = lax.optimization_barrier((partner, near, left, raised))
    raised = lax.ppermute(raised, "space", [(a, (a + 1) % space) for a in range(space)])
    far = around_x(partner)
    left, raised = left.reshape(8 * ROWS, DEPTH), raised.reshape(4 * ROWS, DEPTH)
    chunks = products(half, left, raised, near, far).reshape(space, 8, 12 * ROWS)
    got = lax.all_to_all(chunks, "space", split_axis=0, concat_axis=0, tiled=True)
    total = jnp.sum(got.astype(jnp.float32), axis=0)
    return total.reshape(2, 4, 3, 4, ROWS).transpose(2, 3, 0, 4, 1)


def solution(mesh):
    return jax.shard_map(
        body,
        mesh=mesh,
        in_specs=(
            P("eig", None, None, "space", None),
            P(None, None, None, None, "space", None),
            P(),
        ),
        out_specs=P(None, None, None, "eig", "space"),
        check_vma=False,
    )
```

```python
import math

import jax
import jax.numpy as jnp
from jax import lax
from jax.experimental import pallas as pl
from jax.experimental.pallas import tpu as pltpu
from jax.sharding import PartitionSpec as P

LX = 64
LY = 8
SITES = LX * LY
ROWS = 32
DEPTH = 6 * SITES
VMEM_BYTES = 40 * 1024 * 1024


def moved_across(field):
    lane = lax.broadcasted_iota(jnp.int32, field.shape, 1)
    return jnp.where(
        lane % LX == 0, pltpu.roll(field, SITES - LX + 1, 1), pltpu.roll(field, 1, 1)
    )


def moved_along(field):
    return pltpu.roll(field, LX, 1)


MOVES = (moved_across, moved_along, lambda field: field)


def left_kernel(plane_ref, block_ref, link_ref, left_ref, raised_ref, table_ref):
    row = lax.broadcasted_iota(jnp.int32, (8, SITES), 0) % 4
    site = lax.broadcasted_iota(jnp.int32, (8, SITES), 1)

    def component(k):
        value = jnp.full((8, SITES), plane_ref[3, k], jnp.int32)
        for p in range(3):
            value = jnp.where(row == p, plane_ref[p, k], value)
        return value

    x_frac = ((component(0) * (site % LX)) & (LX - 1)).astype(jnp.float32) / LX
    y_frac = ((component(1) * (site // LX)) & (LY - 1)).astype(jnp.float32) / LY
    extent = plane_ref[4, 1]
    z_frac = ((component(2) * plane_ref[4, 0]) & (extent - 1)).astype(jnp.float32)
    z_frac = z_frac / extent.astype(jnp.float32)
    angles = 2.0 * math.pi * (x_frac + y_frac + z_frac)
    first = lax.broadcasted_iota(jnp.int32, (8, SITES), 0) < 4
    table = jnp.where(first, jnp.cos(angles), jnp.sin(angles))
    for d in range(3):
        table_ref[d] = MOVES[d](table)

    def rows_of(group, carry):
        rows = pl.ds(pl.multiple_of(group * 16, 16), 16)
        for d in range(3):
            for out_colour in range(3):
                real_base = jnp.zeros((16, SITES), jnp.float32)
                imag_base = jnp.zeros((16, SITES), jnp.float32)
                for colour in range(3):
                    at = 2 * SITES * colour
                    real_vec = block_ref[rows, at : at + SITES].astype(jnp.float32)
                    imag_vec = block_ref[rows, at + SITES : at + 2 * SITES].astype(jnp.float32)
                    real_link = link_ref[d, colour, out_colour, 0]
                    imag_link = link_ref[d, colour, out_colour, 1]
                    real_base += real_vec * real_link + imag_vec * imag_link
                    imag_base += real_vec * imag_link - imag_vec * real_link
                real_base, imag_base = MOVES[d](real_base), MOVES[d](imag_base)
                at = 2 * SITES * out_colour
                to_ref, to = (raised_ref, 0) if d == 2 else (left_ref, 4 * d)
                for p in range(4):
                    cosine = table_ref[d, p : p + 1, :]
                    sine = table_ref[d, p + 4 : p + 5, :]
                    to_ref[to + p, rows, at : at + SITES] = (
                        real_base * cosine + imag_base * sine
                    ).astype(jnp.bfloat16)
                    to_ref[to + p, rows, at + SITES : at + 2 * SITES] = (
                        imag_base * cosine - real_base * sine
                    ).astype(jnp.bfloat16)
        return carry

    lax.fori_loop(0, ROWS // 16, rows_of, 0)


def left_operand(plane, block, links):
    return pl.pallas_call(
        left_kernel,
        out_shape=[
            jax.ShapeDtypeStruct((8, ROWS, DEPTH), jnp.bfloat16),
            jax.ShapeDtypeStruct((4, ROWS, DEPTH), jnp.bfloat16),
        ],
        in_specs=[pl.BlockSpec(memory_space=pltpu.SMEM)]
        + [pl.BlockSpec(memory_space=pltpu.VMEM)] * 2,
        out_specs=[pl.BlockSpec(memory_space=pltpu.VMEM)] * 2,
        scratch_shapes=[pltpu.VMEM((3, 8, SITES), jnp.float32)],
        compiler_params=pltpu.CompilerParams(vmem_limit_bytes=VMEM_BYTES),
    )(plane, block, links)


def product_kernel(where_ref, left_ref, raised_ref, *refs):
    near_refs, (far_ref, out_ref, both_ref) = refs[:4], refs[4:]

    def spread(source_ref, to, rows):
        for colour in range(3):
            at = 2 * SITES * colour
            real_vec = source_ref[:, at : at + SITES]
            imag_vec = source_ref[:, at + SITES : at + 2 * SITES]
            both_ref[to : to + rows, at : at + SITES] = real_vec
            both_ref[to : to + rows, at + SITES : at + 2 * SITES] = -imag_vec
            both_ref[to + 128 : to + 128 + rows, at : at + SITES] = imag_vec
            both_ref[to + 128 : to + 128 + rows, at + SITES : at + 2 * SITES] = real_vec

    def multiply(source_ref, half, first, least, most):
        product = lax.dot_general(
            both_ref[...],
            source_ref[...],
            (((1,), (1,)), ((), ())),
            preferred_element_type=jnp.float32,
        )
        width = most - least
        real_part = product[0:128].reshape(16, 8, width)
        imag_part = product[128:256].reshape(16, 8, width)
        upper = lax.broadcasted_iota(jnp.int32, (16, 8, width), 1) < 4
        even = jnp.where(upper, real_part, pltpu.roll(imag_part, 4, 1)).astype(jnp.bfloat16)
        odd = jnp.where(upper, pltpu.roll(real_part, 4, 1), imag_part).astype(jnp.bfloat16)
        for block in range(4):
            for pair in range(4):
                out_ref[first ^ block, half, 2 * pair, :, least:most] = even[4 * block + pair]
                out_ref[first ^ block, half, 2 * pair + 1, :, least:most] = odd[4 * block + pair]

    def multiply_all(half, first):
        multiply(left_ref, half, first, 0, 8 * ROWS)
        multiply(raised_ref, half, first, 8 * ROWS, 12 * ROWS)

    half = where_ref[0]
    for block in range(4):
        spread(near_refs[block], ROWS * block, ROWS)
    multiply_all(half, where_ref[1])
    spread(far_ref, 0, 128)
    multiply_all(1 - half, 0)


def products(where, left, raised, near, far):
    return pl.pallas_call(
        product_kernel,
        out_shape=jax.ShapeDtypeStruct((4, 2, 8, 8, 12 * ROWS), jnp.bfloat16),
        in_specs=[pl.BlockSpec(memory_space=pltpu.SMEM)]
        + [pl.BlockSpec(memory_space=pltpu.VMEM)] * 7,
        out_specs=pl.BlockSpec(memory_space=pltpu.VMEM),
        scratch_shapes=[pltpu.VMEM((256, DEPTH), jnp.bfloat16)],
        compiler_params=pltpu.CompilerParams(vmem_limit_bytes=VMEM_BYTES),
    )(where, left, raised, *near, far)


def body(eigenvectors, gauge_links, momenta):
    space = lax.axis_size("space")
    eig = lax.axis_size("eig")
    s = lax.axis_index("space")
    e = lax.axis_index("eig")
    block = eigenvectors.reshape(ROWS, DEPTH)
    row = lax.broadcasted_iota(jnp.int32, (5, 3), 0)
    column = lax.broadcasted_iota(jnp.int32, (5, 3), 1)
    plane = jnp.where(column == 0, s, space).astype(jnp.int32)
    plane = jnp.where(row < 4, jnp.pad(momenta, ((0, 1), (0, 0))), plane)
    where = jnp.stack([e & 1, e >> 1]).astype(jnp.int32)
    groups = [list(range(0, eig, 2)), list(range(1, eig, 2))]

    def swapped(value, bits):
        return lax.ppermute(value, "eig", [(a, a ^ bits) for a in range(eig)])

    partner = swapped(block, 1)
    first = swapped(block, 2)
    third = swapped(block, 6)
    left, raised = left_operand(plane, block, gauge_links)
    left, raised, first = lax.optimization_barrier((left, raised, first))
    second = swapped(first, 6)
    partner, first, second, third, raised = lax.optimization_barrier(
        (partner, first, second, third, raised)
    )
    raised = lax.ppermute(raised, "space", [(a, (a + 1) % space) for a in range(space)])
    far = lax.all_gather(partner, "eig", axis_index_groups=groups, tiled=True)
    left, raised = left.reshape(8 * ROWS, DEPTH), raised.reshape(4 * ROWS, DEPTH)
    near = (block, first, second, third)
    chunks = products(where, left, raised, near, far).reshape(space, 8, 12 * ROWS)
    got = lax.all_to_all(chunks, "space", split_axis=0, concat_axis=0, tiled=True)
    total = jnp.sum(got.astype(jnp.float32), axis=0)
    return total.reshape(2, 4, 3, 4, ROWS).transpose(2, 3, 0, 4, 1)


def solution(mesh):
    return jax.shard_map(
        body,
        mesh=mesh,
        in_specs=(
            P("eig", None, None, "space", None),
            P(None, None, None, None, "space", None),
            P(),
        ),
        out_specs=P(None, None, None, "eig", "space"),
        check_vma=False,
    )
```

```python
import math

import jax
import jax.numpy as jnp
from jax import lax
from jax.experimental import pallas as pl
from jax.experimental.pallas import tpu as pltpu
from jax.sharding import PartitionSpec as P

LX = 64
LY = 8
SITES = LX * LY
ROWS = 32
DEPTH = 6 * SITES
VMEM_BYTES = 40 * 1024 * 1024


def moved_across(field):
    lane = lax.broadcasted_iota(jnp.int32, field.shape, 1)
    return jnp.where(
        lane % LX == 0, pltpu.roll(field, SITES - LX + 1, 1), pltpu.roll(field, 1, 1)
    )


def moved_along(field):
    return pltpu.roll(field, LX, 1)


MOVES = (moved_across, moved_along, lambda field: field)


def left_kernel(plane_ref, block_ref, link_ref, left_ref, raised_ref, table_ref):
    row = lax.broadcasted_iota(jnp.int32, (8, SITES), 0) % 4
    site = lax.broadcasted_iota(jnp.int32, (8, SITES), 1)

    def component(k):
        value = jnp.full((8, SITES), plane_ref[3, k], jnp.int32)
        for p in range(3):
            value = jnp.where(row == p, plane_ref[p, k], value)
        return value

    x_frac = ((component(0) * (site % LX)) & (LX - 1)).astype(jnp.float32) / LX
    y_frac = ((component(1) * (site // LX)) & (LY - 1)).astype(jnp.float32) / LY
    extent = plane_ref[4, 1]
    z_frac = ((component(2) * plane_ref[4, 0]) & (extent - 1)).astype(jnp.float32)
    z_frac = z_frac / extent.astype(jnp.float32)
    angles = 2.0 * math.pi * (x_frac + y_frac + z_frac)
    first = lax.broadcasted_iota(jnp.int32, (8, SITES), 0) < 4
    table = jnp.where(first, jnp.cos(angles), jnp.sin(angles))
    for d in range(3):
        table_ref[d] = MOVES[d](table)

    def rows_of(group, carry):
        rows = pl.ds(pl.multiple_of(group * 16, 16), 16)
        for d in range(3):
            for out_colour in range(3):
                real_base = jnp.zeros((16, SITES), jnp.float32)
                imag_base = jnp.zeros((16, SITES), jnp.float32)
                for colour in range(3):
                    at = 2 * SITES * colour
                    real_vec = block_ref[rows, at : at + SITES].astype(jnp.float32)
                    imag_vec = block_ref[rows, at + SITES : at + 2 * SITES].astype(jnp.float32)
                    real_link = link_ref[d, colour, out_colour, 0]
                    imag_link = link_ref[d, colour, out_colour, 1]
                    real_base += real_vec * real_link + imag_vec * imag_link
                    imag_base += real_vec * imag_link - imag_vec * real_link
                real_base, imag_base = MOVES[d](real_base), MOVES[d](imag_base)
                at = 2 * SITES * out_colour
                to_ref, to = (raised_ref, 0) if d == 2 else (left_ref, 4 * d)
                for p in range(4):
                    cosine = table_ref[d, p : p + 1, :]
                    sine = table_ref[d, p + 4 : p + 5, :]
                    to_ref[to + p, rows, at : at + SITES] = (
                        real_base * cosine + imag_base * sine
                    ).astype(jnp.bfloat16)
                    to_ref[to + p, rows, at + SITES : at + 2 * SITES] = (
                        imag_base * cosine - real_base * sine
                    ).astype(jnp.bfloat16)
        return carry

    lax.fori_loop(0, ROWS // 16, rows_of, 0)


def left_operand(plane, block, links):
    return pl.pallas_call(
        left_kernel,
        out_shape=[
            jax.ShapeDtypeStruct((8, ROWS, DEPTH), jnp.bfloat16),
            jax.ShapeDtypeStruct((4, ROWS, DEPTH), jnp.bfloat16),
        ],
        in_specs=[pl.BlockSpec(memory_space=pltpu.SMEM)]
        + [pl.BlockSpec(memory_space=pltpu.VMEM)] * 2,
        out_specs=[pl.BlockSpec(memory_space=pltpu.VMEM)] * 2,
        scratch_shapes=[pltpu.VMEM((3, 8, SITES), jnp.float32)],
        compiler_params=pltpu.CompilerParams(vmem_limit_bytes=VMEM_BYTES),
    )(plane, block, links)


def product_kernel(half_ref, left_ref, raised_ref, near_ref, far_ref, out_ref, both_ref):
    def spread(source_ref):
        for colour in range(3):
            at = 2 * SITES * colour
            real_vec = source_ref[:, at : at + SITES]
            imag_vec = source_ref[:, at + SITES : at + 2 * SITES]
            both_ref[0:128, at : at + SITES] = real_vec
            both_ref[0:128, at + SITES : at + 2 * SITES] = -imag_vec
            both_ref[128:256, at : at + SITES] = imag_vec
            both_ref[128:256, at + SITES : at + 2 * SITES] = real_vec

    def multiply(source_ref, half, least, most):
        product = lax.dot_general(
            both_ref[...],
            source_ref[...],
            (((1,), (1,)), ((), ())),
            preferred_element_type=jnp.float32,
        )
        width = most - least
        real_part = product[0:128].reshape(16, 8, width)
        imag_part = product[128:256].reshape(16, 8, width)
        upper = lax.broadcasted_iota(jnp.int32, (16, 8, width), 1) < 4
        even = jnp.where(upper, real_part, pltpu.roll(imag_part, 4, 1)).astype(jnp.bfloat16)
        odd = jnp.where(upper, pltpu.roll(real_part, 4, 1), imag_part).astype(jnp.bfloat16)
        for block in range(4):
            for pair in range(4):
                out_ref[block, half, 2 * pair, :, least:most] = even[4 * block + pair]
                out_ref[block, half, 2 * pair + 1, :, least:most] = odd[4 * block + pair]

    for source_ref, half in ((near_ref, half_ref[0]), (far_ref, 1 - half_ref[0])):
        spread(source_ref)
        multiply(left_ref, half, 0, 8 * ROWS)
        multiply(raised_ref, half, 8 * ROWS, 12 * ROWS)


def products(half, left, raised, near, far):
    return pl.pallas_call(
        product_kernel,
        out_shape=jax.ShapeDtypeStruct((4, 2, 8, 8, 12 * ROWS), jnp.bfloat16),
        in_specs=[pl.BlockSpec(memory_space=pltpu.SMEM)]
        + [pl.BlockSpec(memory_space=pltpu.VMEM)] * 4,
        out_specs=pl.BlockSpec(memory_space=pltpu.VMEM),
        scratch_shapes=[pltpu.VMEM((256, DEPTH), jnp.bfloat16)],
        compiler_params=pltpu.CompilerParams(vmem_limit_bytes=VMEM_BYTES),
    )(half, left, raised, near, far)


def body(eigenvectors, gauge_links, momenta):
    space = lax.axis_size("space")
    eig = lax.axis_size("eig")
    s = lax.axis_index("space")
    e = lax.axis_index("eig")
    block = eigenvectors.reshape(ROWS, DEPTH)
    row = lax.broadcasted_iota(jnp.int32, (5, 3), 0)
    column = lax.broadcasted_iota(jnp.int32, (5, 3), 1)
    plane = jnp.where(column == 0, s, space).astype(jnp.int32)
    plane = jnp.where(row < 4, jnp.pad(momenta, ((0, 1), (0, 0))), plane)
    half = (e & 1).astype(jnp.int32).reshape(1)
    groups = [list(range(0, eig, 2)), list(range(1, eig, 2))]

    def around_x(value):
        copies = jnp.broadcast_to(value[None], (eig // 2, ROWS, DEPTH))
        blocks = lax.all_to_all(
            copies, "eig", split_axis=0, concat_axis=0, axis_index_groups=groups, tiled=True
        )
        return blocks.reshape(eig // 2 * ROWS, DEPTH)

    partner = lax.ppermute(block, "eig", [(a, a ^ 1) for a in range(eig)])
    near = around_x(block)
    near, plane = lax.optimization_barrier((near, plane))
    left, raised = left_operand(plane, block, gauge_links)

    partner, near, left, raised = lax.optimization_barrier((partner, near, left, raised))
    raised = lax.ppermute(raised, "space", [(a, (a + 1) % space) for a in range(space)])
    far = around_x(partner)
    left, raised = left.reshape(8 * ROWS, DEPTH), raised.reshape(4 * ROWS, DEPTH)
    chunks = products(half, left, raised, near, far).reshape(space, 8, 12 * ROWS)
    got = lax.all_to_all(chunks, "space", split_axis=0, concat_axis=0, tiled=True)
    total = jnp.sum(got.astype(jnp.float32), axis=0)
    return total.reshape(2, 4, 3, 4, ROWS).transpose(2, 3, 0, 4, 1)


def solution(mesh):
    return jax.shard_map(
        body,
        mesh=mesh,
        in_specs=(
            P("eig", None, None, "space", None),
            P(None, None, None, None, "space", None),
            P(),
        ),
        out_specs=P(None, None, None, "eig", "space"),
        check_vma=False,
    )
```

```python
import math

import jax
import jax.numpy as jnp
from jax import lax
from jax.experimental import pallas as pl
from jax.experimental.pallas import tpu as pltpu
from jax.sharding import PartitionSpec as P

LX = 64
LY = 8
SITES = LX * LY
ROWS = 32
DEPTH = 6 * SITES
VMEM_BYTES = 40 * 1024 * 1024


def moved_across(field):
    lane = lax.broadcasted_iota(jnp.int32, field.shape, 1)
    return jnp.where(
        lane % LX == 0, pltpu.roll(field, SITES - LX + 1, 1), pltpu.roll(field, 1, 1)
    )


def moved_along(field):
    return pltpu.roll(field, LX, 1)


MOVES = (moved_across, moved_along, lambda field: field)


def left_kernel(plane_ref, block_ref, link_ref, left_ref, raised_ref, table_ref):
    row = lax.broadcasted_iota(jnp.int32, (8, SITES), 0) % 4
    site = lax.broadcasted_iota(jnp.int32, (8, SITES), 1)

    def component(k):
        value = jnp.full((8, SITES), plane_ref[3, k], jnp.int32)
        for p in range(3):
            value = jnp.where(row == p, plane_ref[p, k], value)
        return value

    x_frac = ((component(0) * (site % LX)) & (LX - 1)).astype(jnp.float32) / LX
    y_frac = ((component(1) * (site // LX)) & (LY - 1)).astype(jnp.float32) / LY
    extent = plane_ref[4, 1]
    z_frac = ((component(2) * plane_ref[4, 0]) & (extent - 1)).astype(jnp.float32)
    z_frac = z_frac / extent.astype(jnp.float32)
    angles = 2.0 * math.pi * (x_frac + y_frac + z_frac)
    first = lax.broadcasted_iota(jnp.int32, (8, SITES), 0) < 4
    table = jnp.where(first, jnp.cos(angles), jnp.sin(angles))
    for d in range(3):
        table_ref[d] = MOVES[d](table)

    def rows_of(group, carry):
        rows = pl.ds(pl.multiple_of(group * 16, 16), 16)
        for d in range(3):
            for out_colour in range(3):
                real_base = jnp.zeros((16, SITES), jnp.float32)
                imag_base = jnp.zeros((16, SITES), jnp.float32)
                for colour in range(3):
                    at = 2 * SITES * colour
                    real_vec = block_ref[rows, at : at + SITES].astype(jnp.float32)
                    imag_vec = block_ref[rows, at + SITES : at + 2 * SITES].astype(jnp.float32)
                    real_link = link_ref[d, colour, out_colour, 0]
                    imag_link = link_ref[d, colour, out_colour, 1]
                    real_base += real_vec * real_link + imag_vec * imag_link
                    imag_base += real_vec * imag_link - imag_vec * real_link
                real_base, imag_base = MOVES[d](real_base), MOVES[d](imag_base)
                at = 2 * SITES * out_colour
                to_ref, to = (raised_ref, 0) if d == 2 else (left_ref, 4 * d)
                for p in range(4):
                    cosine = table_ref[d, p : p + 1, :]
                    sine = table_ref[d, p + 4 : p + 5, :]
                    to_ref[to + p, rows, at : at + SITES] = (
                        real_base * cosine + imag_base * sine
                    ).astype(jnp.bfloat16)
                    to_ref[to + p, rows, at + SITES : at + 2 * SITES] = (
                        imag_base * cosine - real_base * sine
                    ).astype(jnp.bfloat16)
        return carry

    lax.fori_loop(0, ROWS // 16, rows_of, 0)


def left_operand(plane, block, links):
    return pl.pallas_call(
        left_kernel,
        out_shape=[
            jax.ShapeDtypeStruct((8, ROWS, DEPTH), jnp.bfloat16),
            jax.ShapeDtypeStruct((4, ROWS, DEPTH), jnp.bfloat16),
        ],
        in_specs=[pl.BlockSpec(memory_space=pltpu.SMEM)]
        + [pl.BlockSpec(memory_space=pltpu.VMEM)] * 2,
        out_specs=[pl.BlockSpec(memory_space=pltpu.VMEM)] * 2,
        scratch_shapes=[pltpu.VMEM((3, 8, SITES), jnp.float32)],
        compiler_params=pltpu.CompilerParams(vmem_limit_bytes=VMEM_BYTES),
    )(plane, block, links)


def multiply_blocks(left_ref, raised_ref, source_ref, both_ref, store):
    def spread():
        for colour in range(3):
            at = 2 * SITES * colour
            real_vec = source_ref[:, at : at + SITES]
            imag_vec = source_ref[:, at + SITES : at + 2 * SITES]
            both_ref[0:128, at : at + SITES] = real_vec
            both_ref[0:128, at + SITES : at + 2 * SITES] = -imag_vec
            both_ref[128:256, at : at + SITES] = imag_vec
            both_ref[128:256, at + SITES : at + 2 * SITES] = real_vec

    def multiply(operand_ref, least, most):
        product = lax.dot_general(
            both_ref[...],
            operand_ref[...],
            (((1,), (1,)), ((), ())),
            preferred_element_type=jnp.float32,
        )
        width = most - least
        real_part = product[0:128].reshape(16, 8, width)
        imag_part = product[128:256].reshape(16, 8, width)
        upper = lax.broadcasted_iota(jnp.int32, (16, 8, width), 1) < 4
        even = jnp.where(upper, real_part, pltpu.roll(imag_part, 4, 1)).astype(jnp.bfloat16)
        odd = jnp.where(upper, pltpu.roll(real_part, 4, 1), imag_part).astype(jnp.bfloat16)
        for block in range(4):
            for pair in range(4):
                store(block, 2 * pair, slice(least, most), even[4 * block + pair])
                store(block, 2 * pair + 1, slice(least, most), odd[4 * block + pair])

    spread()
    multiply(left_ref, 0, 8 * ROWS)
    multiply(raised_ref, 8 * ROWS, 12 * ROWS)


def near_kernel(left_ref, raised_ref, near_ref, out_ref, both_ref):
    def store(block, low, lanes, value):
        out_ref[block, low, :, lanes] = value

    multiply_blocks(left_ref, raised_ref, near_ref, both_ref, store)


def far_kernel(half_ref, left_ref, raised_ref, far_ref, part_ref, out_ref, both_ref):
    half = half_ref[0]

    def store(block, low, lanes, value):
        out_ref[block, 1 - half, low, :, lanes] = value

    for block in range(4):
        out_ref[block, half] = part_ref[block]
    multiply_blocks(left_ref, raised_ref, far_ref, both_ref, store)


def product_call(kernel, shape, scalars, *arrays):
    return pl.pallas_call(
        kernel,
        out_shape=jax.ShapeDtypeStruct(shape, jnp.bfloat16),
        in_specs=[pl.BlockSpec(memory_space=pltpu.SMEM)] * len(scalars)
        + [pl.BlockSpec(memory_space=pltpu.VMEM)] * len(arrays),
        out_specs=pl.BlockSpec(memory_space=pltpu.VMEM),
        scratch_shapes=[pltpu.VMEM((256, DEPTH), jnp.bfloat16)],
        compiler_params=pltpu.CompilerParams(vmem_limit_bytes=VMEM_BYTES),
    )(*scalars, *arrays)


def body(eigenvectors, gauge_links, momenta):
    space = lax.axis_size("space")
    eig = lax.axis_size("eig")
    s = lax.axis_index("space")
    e = lax.axis_index("eig")
    block = eigenvectors.reshape(ROWS, DEPTH)
    row = lax.broadcasted_iota(jnp.int32, (5, 3), 0)
    column = lax.broadcasted_iota(jnp.int32, (5, 3), 1)
    plane = jnp.where(column == 0, s, space).astype(jnp.int32)
    plane = jnp.where(row < 4, jnp.pad(momenta, ((0, 1), (0, 0))), plane)
    half = (e & 1).astype(jnp.int32).reshape(1)
    groups = [list(range(0, eig, 2)), list(range(1, eig, 2))]

    def around_x(value):
        copies = jnp.broadcast_to(value[None], (eig // 2, ROWS, DEPTH))
        blocks = lax.all_to_all(
            copies, "eig", split_axis=0, concat_axis=0, axis_index_groups=groups, tiled=True
        )
        return blocks.reshape(eig // 2 * ROWS, DEPTH)

    partner = lax.ppermute(block, "eig", [(a, a ^ 1) for a in range(eig)])
    near = around_x(block)
    left, raised = left_operand(plane, block, gauge_links)

    partner, left, raised = lax.optimization_barrier((partner, left, raised))
    raised = lax.ppermute(raised, "space", [(a, (a + 1) % space) for a in range(space)])
    far = around_x(partner)
    left, raised = left.reshape(8 * ROWS, DEPTH), raised.reshape(4 * ROWS, DEPTH)
    part = product_call(near_kernel, (4, 8, 8, 12 * ROWS), (), left, raised, near)
    chunks = product_call(
        far_kernel, (4, 2, 8, 8, 12 * ROWS), (half,), left, raised, far, part
    ).reshape(space, 8, 12 * ROWS)
    got = lax.all_to_all(chunks, "space", split_axis=0, concat_axis=0, tiled=True)
    total = jnp.sum(got.astype(jnp.float32), axis=0)
    return total.reshape(2, 4, 3, 4, ROWS).transpose(2, 3, 0, 4, 1)


def solution(mesh):
    return jax.shard_map(
        body,
        mesh=mesh,
        in_specs=(
            P("eig", None, None, "space", None),
            P(None, None, None, None, "space", None),
            P(),
        ),
        out_specs=P(None, None, None, "eig", "space"),
        check_vma=False,
    )
```

```python
import math

import jax
import jax.numpy as jnp
from jax import lax
from jax.experimental import pallas as pl
from jax.experimental.pallas import tpu as pltpu
from jax.sharding import PartitionSpec as P

LX = 64
LY = 8
SITES = LX * LY
ROWS = 32
DEPTH = 6 * SITES
VMEM_BYTES = 40 * 1024 * 1024


def moved_across(field):
    lane = lax.broadcasted_iota(jnp.int32, field.shape, 1)
    return jnp.where(
        lane % LX == 0, pltpu.roll(field, SITES - LX + 1, 1), pltpu.roll(field, 1, 1)
    )


def moved_along(field):
    return pltpu.roll(field, LX, 1)


MOVES = (moved_across, moved_along, lambda field: field)


def left_kernel(plane_ref, block_ref, link_ref, left_ref, raised_ref, table_ref):
    row = lax.broadcasted_iota(jnp.int32, (8, SITES), 0) % 4
    site = lax.broadcasted_iota(jnp.int32, (8, SITES), 1)

    def component(k):
        value = jnp.full((8, SITES), plane_ref[3, k], jnp.int32)
        for p in range(3):
            value = jnp.where(row == p, plane_ref[p, k], value)
        return value

    x_frac = ((component(0) * (site % LX)) & (LX - 1)).astype(jnp.float32) / LX
    y_frac = ((component(1) * (site // LX)) & (LY - 1)).astype(jnp.float32) / LY
    extent = plane_ref[4, 1]
    z_frac = ((component(2) * plane_ref[4, 0]) & (extent - 1)).astype(jnp.float32)
    z_frac = z_frac / extent.astype(jnp.float32)
    angles = 2.0 * math.pi * (x_frac + y_frac + z_frac)
    first = lax.broadcasted_iota(jnp.int32, (8, SITES), 0) < 4
    table = jnp.where(first, jnp.cos(angles), jnp.sin(angles))
    for d in range(3):
        table_ref[d] = MOVES[d](table)

    def rows_of(group, carry):
        rows = pl.ds(pl.multiple_of(group * 16, 16), 16)
        for d in range(3):
            for out_colour in range(3):
                real_base = jnp.zeros((16, SITES), jnp.float32)
                imag_base = jnp.zeros((16, SITES), jnp.float32)
                for colour in range(3):
                    at = 2 * SITES * colour
                    real_vec = block_ref[rows, at : at + SITES].astype(jnp.float32)
                    imag_vec = block_ref[rows, at + SITES : at + 2 * SITES].astype(jnp.float32)
                    real_link = link_ref[d, colour, out_colour, 0]
                    imag_link = link_ref[d, colour, out_colour, 1]
                    real_base += real_vec * real_link + imag_vec * imag_link
                    imag_base += real_vec * imag_link - imag_vec * real_link
                real_base, imag_base = MOVES[d](real_base), MOVES[d](imag_base)
                at = 2 * SITES * out_colour
                to_ref, to = (raised_ref, 0) if d == 2 else (left_ref, 4 * d)
                for p in range(4):
                    cosine = table_ref[d, p : p + 1, :]
                    sine = table_ref[d, p + 4 : p + 5, :]
                    to_ref[to + p, rows, at : at + SITES] = (
                        real_base * cosine + imag_base * sine
                    ).astype(jnp.bfloat16)
                    to_ref[to + p, rows, at + SITES : at + 2 * SITES] = (
                        imag_base * cosine - real_base * sine
                    ).astype(jnp.bfloat16)
        return carry

    lax.fori_loop(0, ROWS // 16, rows_of, 0)


def left_operand(plane, block, links):
    return pl.pallas_call(
        left_kernel,
        out_shape=[
            jax.ShapeDtypeStruct((8, ROWS, DEPTH), jnp.bfloat16),
            jax.ShapeDtypeStruct((4, ROWS, DEPTH), jnp.bfloat16),
        ],
        in_specs=[pl.BlockSpec(memory_space=pltpu.SMEM)]
        + [pl.BlockSpec(memory_space=pltpu.VMEM)] * 2,
        out_specs=[pl.BlockSpec(memory_space=pltpu.VMEM)] * 2,
        scratch_shapes=[pltpu.VMEM((3, 8, SITES), jnp.float32)],
        compiler_params=pltpu.CompilerParams(vmem_limit_bytes=VMEM_BYTES),
    )(plane, block, links)


def product_kernel(half_ref, left_ref, raised_ref, near_ref, far_ref, out_ref, both_ref):
    def spread(source_ref):
        for colour in range(3):
            at = 2 * SITES * colour
            real_vec = source_ref[:, at : at + SITES]
            imag_vec = source_ref[:, at + SITES : at + 2 * SITES]
            both_ref[0:128, at : at + SITES] = real_vec
            both_ref[0:128, at + SITES : at + 2 * SITES] = -imag_vec
            both_ref[128:256, at : at + SITES] = imag_vec
            both_ref[128:256, at + SITES : at + 2 * SITES] = real_vec

    def multiply(source_ref, half, least, most):
        product = lax.dot_general(
            both_ref[...],
            source_ref[...],
            (((1,), (1,)), ((), ())),
            preferred_element_type=jnp.float32,
        )
        width = most - least
        real_part = product[0:128].reshape(16, 8, width)
        imag_part = product[128:256].reshape(16, 8, width)
        upper = lax.broadcasted_iota(jnp.int32, (16, 8, width), 1) < 4
        even = jnp.where(upper, real_part, pltpu.roll(imag_part, 4, 1)).astype(jnp.bfloat16)
        odd = jnp.where(upper, pltpu.roll(real_part, 4, 1), imag_part).astype(jnp.bfloat16)
        for block in range(4):
            for pair in range(4):
                out_ref[block, half, 2 * pair, :, least:most] = even[4 * block + pair]
                out_ref[block, half, 2 * pair + 1, :, least:most] = odd[4 * block + pair]

    for source_ref, half in ((near_ref, half_ref[0]), (far_ref, 1 - half_ref[0])):
        spread(source_ref)
        multiply(left_ref, half, 0, 8 * ROWS)
        multiply(raised_ref, half, 8 * ROWS, 12 * ROWS)


def products(half, left, raised, near, far):
    return pl.pallas_call(
        product_kernel,
        out_shape=jax.ShapeDtypeStruct((4, 2, 8, 8, 12 * ROWS), jnp.bfloat16),
        in_specs=[pl.BlockSpec(memory_space=pltpu.SMEM)]
        + [pl.BlockSpec(memory_space=pltpu.VMEM)] * 4,
        out_specs=pl.BlockSpec(memory_space=pltpu.VMEM),
        scratch_shapes=[pltpu.VMEM((256, DEPTH), jnp.bfloat16)],
        compiler_params=pltpu.CompilerParams(vmem_limit_bytes=VMEM_BYTES),
    )(half, left, raised, near, far)


def body(eigenvectors, gauge_links, momenta):
    space = lax.axis_size("space")
    eig = lax.axis_size("eig")
    s = lax.axis_index("space")
    e = lax.axis_index("eig")
    block = eigenvectors.reshape(ROWS, DEPTH)
    row = lax.broadcasted_iota(jnp.int32, (5, 3), 0)
    column = lax.broadcasted_iota(jnp.int32, (5, 3), 1)
    plane = jnp.where(column == 0, s, space).astype(jnp.int32)
    plane = jnp.where(row < 4, jnp.pad(momenta, ((0, 1), (0, 0))), plane)
    half = (e & 1).astype(jnp.int32).reshape(1)
    groups = [list(range(0, eig, 2)), list(range(1, eig, 2))]

    partner = lax.ppermute(block, "eig", [(a, a ^ 1) for a in range(eig)])
    copies = jnp.broadcast_to(block[None], (eig // 2, ROWS, DEPTH))
    near = lax.all_to_all(
        copies, "eig", split_axis=0, concat_axis=0, axis_index_groups=groups, tiled=True
    ).reshape(eig // 2 * ROWS, DEPTH)
    left, raised = left_operand(plane, block, gauge_links)

    partner, left, raised = lax.optimization_barrier((partner, left, raised))
    raised = lax.ppermute(raised, "space", [(a, (a + 1) % space) for a in range(space)])
    partner, near = lax.optimization_barrier((partner, near))
    far = lax.all_gather(partner, "eig", axis_index_groups=groups, tiled=True)
    left, raised = left.reshape(8 * ROWS, DEPTH), raised.reshape(4 * ROWS, DEPTH)
    chunks = products(half, left, raised, near, far).reshape(space, 8, 12 * ROWS)
    got = lax.all_to_all(chunks, "space", split_axis=0, concat_axis=0, tiled=True)
    total = jnp.sum(got.astype(jnp.float32), axis=0)
    return total.reshape(2, 4, 3, 4, ROWS).transpose(2, 3, 0, 4, 1)


def solution(mesh):
    return jax.shard_map(
        body,
        mesh=mesh,
        in_specs=(
            P("eig", None, None, "space", None),
            P(None, None, None, None, "space", None),
            P(),
        ),
        out_specs=P(None, None, None, "eig", "space"),
        check_vma=False,
    )
```

```python
import math

import jax
import jax.numpy as jnp
from jax import lax
from jax.experimental import pallas as pl
from jax.experimental.pallas import tpu as pltpu
from jax.sharding import PartitionSpec as P

LX = 64
LY = 8
SITES = LX * LY
ROWS = 32
DEPTH = 6 * SITES
VMEM_BYTES = 40 * 1024 * 1024


def moved_across(field):
    lane = lax.broadcasted_iota(jnp.int32, field.shape, 1)
    return jnp.where(
        lane % LX == 0, pltpu.roll(field, SITES - LX + 1, 1), pltpu.roll(field, 1, 1)
    )


def moved_along(field):
    return pltpu.roll(field, LX, 1)


MOVES = (moved_across, moved_along, lambda field: field)


def left_kernel(plane_ref, which_ref, block_ref, below_ref, link_ref, link_below_ref, left_ref, table_ref):
    row = lax.broadcasted_iota(jnp.int32, (8, SITES), 0) % 4
    site = lax.broadcasted_iota(jnp.int32, (8, SITES), 1)

    def component(k):
        value = jnp.full((8, SITES), plane_ref[3, k], jnp.int32)
        for p in range(3):
            value = jnp.where(row == p, plane_ref[p, k], value)
        return value

    x_frac = ((component(0) * (site % LX)) & (LX - 1)).astype(jnp.float32) / LX
    y_frac = ((component(1) * (site // LX)) & (LY - 1)).astype(jnp.float32) / LY
    extent = plane_ref[4, 1]
    first = lax.broadcasted_iota(jnp.int32, (8, SITES), 0) < 4

    def plane_table(height):
        z_frac = ((component(2) * height) & (extent - 1)).astype(jnp.float32)
        z_frac = z_frac / extent.astype(jnp.float32)
        angles = 2.0 * math.pi * (x_frac + y_frac + z_frac)
        return jnp.where(first, jnp.cos(angles), jnp.sin(angles))

    here = plane_table(plane_ref[4, 0])
    table_ref[0] = moved_across(here)
    table_ref[1] = moved_along(here)
    table_ref[2] = plane_table((plane_ref[4, 0] - 1) & (extent - 1))

    here_ref = block_ref.at[which_ref[0]] if len(block_ref.shape) == 3 else block_ref

    def rows_of(group, carry):
        rows = pl.ds(pl.multiple_of(group * 16, 16), 16)
        for d in range(3):
            source_ref = below_ref if d == 2 else here_ref
            for out_colour in range(3):
                real_base = jnp.zeros((16, SITES), jnp.float32)
                imag_base = jnp.zeros((16, SITES), jnp.float32)
                for colour in range(3):
                    at = 2 * SITES * colour
                    real_vec = source_ref[rows, at : at + SITES].astype(jnp.float32)
                    imag_vec = source_ref[rows, at + SITES : at + 2 * SITES].astype(jnp.float32)
                    if d == 2:
                        real_link = link_below_ref[2, colour, out_colour, 0]
                        imag_link = link_below_ref[2, colour, out_colour, 1]
                    else:
                        real_link = link_ref[d, colour, out_colour, 0]
                        imag_link = link_ref[d, colour, out_colour, 1]
                    real_base += real_vec * real_link + imag_vec * imag_link
                    imag_base += real_vec * imag_link - imag_vec * real_link
                real_base, imag_base = MOVES[d](real_base), MOVES[d](imag_base)
                at = 2 * SITES * out_colour
                for p in range(4):
                    cosine = table_ref[d, p : p + 1, :]
                    sine = table_ref[d, p + 4 : p + 5, :]
                    left_ref[4 * d + p, rows, at : at + SITES] = (
                        real_base * cosine + imag_base * sine
                    ).astype(jnp.bfloat16)
                    left_ref[4 * d + p, rows, at + SITES : at + 2 * SITES] = (
                        imag_base * cosine - real_base * sine
                    ).astype(jnp.bfloat16)
        return carry

    lax.fori_loop(0, ROWS // 16, rows_of, 0)


def left_operand(plane, which, blocks, below, links, links_below):
    return pl.pallas_call(
        left_kernel,
        out_shape=jax.ShapeDtypeStruct((12, ROWS, DEPTH), jnp.bfloat16),
        in_specs=[pl.BlockSpec(memory_space=pltpu.SMEM)] * 2
        + [pl.BlockSpec(memory_space=pltpu.VMEM)] * 4,
        out_specs=pl.BlockSpec(memory_space=pltpu.VMEM),
        scratch_shapes=[pltpu.VMEM((3, 8, SITES), jnp.float32)],
        compiler_params=pltpu.CompilerParams(vmem_limit_bytes=VMEM_BYTES),
    )(plane, which, blocks, below, links, links_below)


def product_kernel(where_ref, own_ref, other_ref, near_ref, far_ref, far_next_ref, out_ref, both_ref):
    def spread(source_ref, to, shift, rows):
        real_rows = slice(to, to + rows)
        imag_rows = slice(to + shift, to + shift + rows)
        for colour in range(3):
            at = 2 * SITES * colour
            real_vec = source_ref[:, at : at + SITES]
            imag_vec = source_ref[:, at + SITES : at + 2 * SITES]
            both_ref[real_rows, at : at + SITES] = real_vec
            both_ref[real_rows, at + SITES : at + 2 * SITES] = -imag_vec
            both_ref[imag_rows, at : at + SITES] = imag_vec
            both_ref[imag_rows, at + SITES : at + 2 * SITES] = real_vec

    def multiply(left_ref, columns, half, places):
        product = lax.dot_general(
            both_ref[0 : 2 * columns],
            left_ref[...],
            (((1,), (1,)), ((), ())),
            preferred_element_type=jnp.float32,
        )
        shape = (columns // 8, 8, 12 * ROWS)
        real_part = product[0:columns].reshape(shape)
        imag_part = product[columns : 2 * columns].reshape(shape)
        upper = lax.broadcasted_iota(jnp.int32, shape, 1) < 4
        even = jnp.where(upper, real_part, pltpu.roll(imag_part, 4, 1)).astype(jnp.bfloat16)
        odd = jnp.where(upper, pltpu.roll(real_part, 4, 1), imag_part).astype(jnp.bfloat16)
        for block, place in enumerate(places):
            for pair in range(4):
                out_ref[place, half, 2 * pair] = even[4 * block + pair]
                out_ref[place, half, 2 * pair + 1] = odd[4 * block + pair]

    half, x = where_ref[0], where_ref[1]
    spread(near_ref, 0, 128, 128)
    multiply(own_ref, 128, half, (0, 1, 2, 3))
    spread(far_ref, 0, 64, ROWS)
    spread(far_next_ref, ROWS, 64, ROWS)
    multiply(own_ref, 64, 1 - half, (x, x ^ 3))
    multiply(other_ref, 64, 1 - half, (x ^ 1, x ^ 2))


def products(where, own, other, near, far, far_next):
    return pl.pallas_call(
        product_kernel,
        out_shape=jax.ShapeDtypeStruct((4, 2, 8, 8, 12 * ROWS), jnp.bfloat16),
        in_specs=[pl.BlockSpec(memory_space=pltpu.SMEM)]
        + [pl.BlockSpec(memory_space=pltpu.VMEM)] * 5,
        out_specs=pl.BlockSpec(memory_space=pltpu.VMEM),
        scratch_shapes=[pltpu.VMEM((256, DEPTH), jnp.bfloat16)],
        compiler_params=pltpu.CompilerParams(vmem_limit_bytes=VMEM_BYTES),
    )(where, own, other, near, far, far_next)


def body(eigenvectors, gauge_links, momenta):
    space = lax.axis_size("space")
    eig = lax.axis_size("eig")
    s = lax.axis_index("space")
    e = lax.axis_index("eig")
    block = eigenvectors.reshape(ROWS, DEPTH)
    row = lax.broadcasted_iota(jnp.int32, (5, 3), 0)
    column = lax.broadcasted_iota(jnp.int32, (5, 3), 1)
    plane = jnp.where(column == 0, s, space).astype(jnp.int32)
    plane = jnp.where(row < 4, jnp.pad(momenta, ((0, 1), (0, 0))), plane)
    zh, x = e & 1, e >> 1
    where = jnp.stack([zh, x]).astype(jnp.int32)
    other_x = (x ^ 1).astype(jnp.int32).reshape(1)
    groups = [list(range(0, eig, 2)), list(range(1, eig, 2))]
    everywhere = [(a, b) for a in range(space) for b in range(eig)]

    def at(a, b):
        return a % space * eig + b

    def from_below(value):
        return lax.ppermute(value, "space", [(a, (a + 1) % space) for a in range(space)])

    partner = lax.ppermute(block, "eig", [(a, a ^ 1) for a in range(eig)])
    links_below = from_below(gauge_links)
    later, links_below = lax.optimization_barrier((block, links_below))
    copies = jnp.broadcast_to(later[None], (eig // 2, ROWS, DEPTH))
    near = lax.all_to_all(
        copies, "eig", split_axis=0, concat_axis=0, axis_index_groups=groups, tiled=True
    )
    below = from_below(later)
    below_other = lax.ppermute(
        later, ("space", "eig"), [(at(a, b), at(a + 1, b ^ 2)) for a, b in everywhere]
    )
    own = left_operand(plane, other_x, block, below, gauge_links, links_below)
    partner, own = lax.optimization_barrier((partner, own))
    far = lax.ppermute(partner, "eig", [(a, a ^ 6) for a in range(eig)])
    other = left_operand(plane, other_x, near, below_other, gauge_links, links_below)
    own, other = own.reshape(12 * ROWS, DEPTH), other.reshape(12 * ROWS, DEPTH)
    chunks = products(where, own, other, near.reshape(4 * ROWS, DEPTH), partner, far)
    chunks = chunks.reshape(space, 8, 12 * ROWS)
    got = lax.all_to_all(chunks, "space", split_axis=0, concat_axis=0, tiled=True)
    total = jnp.sum(got.astype(jnp.float32), axis=0)
    y = s // 8
    held = ((y & 1) != zh) & ((y >> 1 != x) & (y >> 1 != x ^ 3))
    pairs = [
        (at(a, b), at(a ^ 16, b ^ 2))
        for a, b in everywhere
        if (a >> 3) & 1 != b & 1 and (a >> 4) not in (b >> 1, (b >> 1) ^ 3)
    ]
    swapped = lax.ppermute(total, ("space", "eig"), pairs)
    total = jnp.where(held, swapped, total)
    return total.reshape(2, 4, 3, 4, ROWS).transpose(2, 3, 0, 4, 1)


def solution(mesh):
    return jax.shard_map(
        body,
        mesh=mesh,
        in_specs=(
            P("eig", None, None, "space", None),
            P(None, None, None, None, "space", None),
            P(),
        ),
        out_specs=P(None, None, None, "eig", "space"),
        check_vma=False,
    )
```

```python
import math

import jax
import jax.numpy as jnp
from jax import lax
from jax.experimental import pallas as pl
from jax.experimental.pallas import tpu as pltpu
from jax.sharding import PartitionSpec as P

LX = 64
LY = 8
SITES = LX * LY
ROWS = 32
DEPTH = 6 * SITES
VMEM_BYTES = 40 * 1024 * 1024


def moved_across(field):
    lane = lax.broadcasted_iota(jnp.int32, field.shape, 1)
    return jnp.where(
        lane % LX == 0, pltpu.roll(field, SITES - LX + 1, 1), pltpu.roll(field, 1, 1)
    )


def moved_along(field):
    return pltpu.roll(field, LX, 1)


MOVES = (moved_across, moved_along, lambda field: field)


def left_kernel(plane_ref, block_ref, link_ref, left_ref, raised_ref, table_ref):
    row = lax.broadcasted_iota(jnp.int32, (8, SITES), 0) % 4
    site = lax.broadcasted_iota(jnp.int32, (8, SITES), 1)

    def component(k):
        value = jnp.full((8, SITES), plane_ref[3, k], jnp.int32)
        for p in range(3):
            value = jnp.where(row == p, plane_ref[p, k], value)
        return value

    x_frac = ((component(0) * (site % LX)) & (LX - 1)).astype(jnp.float32) / LX
    y_frac = ((component(1) * (site // LX)) & (LY - 1)).astype(jnp.float32) / LY
    extent = plane_ref[4, 1]
    z_frac = ((component(2) * plane_ref[4, 0]) & (extent - 1)).astype(jnp.float32)
    z_frac = z_frac / extent.astype(jnp.float32)
    angles = 2.0 * math.pi * (x_frac + y_frac + z_frac)
    first = lax.broadcasted_iota(jnp.int32, (8, SITES), 0) < 4
    table = jnp.where(first, jnp.cos(angles), jnp.sin(angles))
    for d in range(3):
        table_ref[d] = MOVES[d](table)

    def rows_of(group, carry):
        rows = pl.ds(pl.multiple_of(group * 16, 16), 16)
        for d in range(3):
            for out_colour in range(3):
                real_base = jnp.zeros((16, SITES), jnp.float32)
                imag_base = jnp.zeros((16, SITES), jnp.float32)
                for colour in range(3):
                    at = 2 * SITES * colour
                    real_vec = block_ref[rows, at : at + SITES].astype(jnp.float32)
                    imag_vec = block_ref[rows, at + SITES : at + 2 * SITES].astype(jnp.float32)
                    real_link = link_ref[d, colour, out_colour, 0]
                    imag_link = link_ref[d, colour, out_colour, 1]
                    real_base += real_vec * real_link + imag_vec * imag_link
                    imag_base += real_vec * imag_link - imag_vec * real_link
                real_base, imag_base = MOVES[d](real_base), MOVES[d](imag_base)
                at = 2 * SITES * out_colour
                to_ref, to = (raised_ref, 0) if d == 2 else (left_ref, 4 * d)
                for p in range(4):
                    cosine = table_ref[d, p : p + 1, :]
                    sine = table_ref[d, p + 4 : p + 5, :]
                    to_ref[to + p, rows, at : at + SITES] = (
                        real_base * cosine + imag_base * sine
                    ).astype(jnp.bfloat16)
                    to_ref[to + p, rows, at + SITES : at + 2 * SITES] = (
                        imag_base * cosine - real_base * sine
                    ).astype(jnp.bfloat16)
        return carry

    lax.fori_loop(0, ROWS // 16, rows_of, 0)


def left_operand(plane, block, links):
    return pl.pallas_call(
        left_kernel,
        out_shape=[
            jax.ShapeDtypeStruct((8, ROWS, DEPTH), jnp.bfloat16),
            jax.ShapeDtypeStruct((4, ROWS, DEPTH), jnp.bfloat16),
        ],
        in_specs=[pl.BlockSpec(memory_space=pltpu.SMEM)]
        + [pl.BlockSpec(memory_space=pltpu.VMEM)] * 2,
        out_specs=[pl.BlockSpec(memory_space=pltpu.VMEM)] * 2,
        scratch_shapes=[pltpu.VMEM((3, 8, SITES), jnp.float32)],
        compiler_params=pltpu.CompilerParams(vmem_limit_bytes=VMEM_BYTES),
    )(plane, block, links)


def product_kernel(half_ref, left_ref, raised_ref, near_ref, far_ref, out_ref, both_ref):
    def spread(source_ref, to):
        real_rows, imag_rows = slice(to, to + 128), slice(to + 256, to + 384)
        for colour in range(3):
            at = 2 * SITES * colour
            real_vec = source_ref[:, at : at + SITES]
            imag_vec = source_ref[:, at + SITES : at + 2 * SITES]
            both_ref[real_rows, at : at + SITES] = real_vec
            both_ref[real_rows, at + SITES : at + 2 * SITES] = -imag_vec
            both_ref[imag_rows, at : at + SITES] = imag_vec
            both_ref[imag_rows, at + SITES : at + 2 * SITES] = real_vec

    def multiply(source_ref, least, most):
        product = lax.dot_general(
            both_ref[...],
            source_ref[...],
            (((1,), (1,)), ((), ())),
            preferred_element_type=jnp.float32,
        )
        width = most - least
        real_part = product[0:256].reshape(32, 8, width)
        imag_part = product[256:512].reshape(32, 8, width)
        upper = lax.broadcasted_iota(jnp.int32, (32, 8, width), 1) < 4
        even = jnp.where(upper, real_part, pltpu.roll(imag_part, 4, 1)).astype(jnp.bfloat16)
        odd = jnp.where(upper, pltpu.roll(real_part, 4, 1), imag_part).astype(jnp.bfloat16)
        for block in range(8):
            half = half_ref[0] if block < 4 else 1 - half_ref[0]
            for pair in range(4):
                out_ref[block % 4, half, 2 * pair, :, least:most] = even[4 * block + pair]
                out_ref[block % 4, half, 2 * pair + 1, :, least:most] = odd[4 * block + pair]

    spread(near_ref, 0)
    spread(far_ref, 128)
    multiply(left_ref, 0, 8 * ROWS)
    multiply(raised_ref, 8 * ROWS, 12 * ROWS)


def products(half, left, raised, near, far):
    return pl.pallas_call(
        product_kernel,
        out_shape=jax.ShapeDtypeStruct((4, 2, 8, 8, 12 * ROWS), jnp.bfloat16),
        in_specs=[pl.BlockSpec(memory_space=pltpu.SMEM)]
        + [pl.BlockSpec(memory_space=pltpu.VMEM)] * 4,
        out_specs=pl.BlockSpec(memory_space=pltpu.VMEM),
        scratch_shapes=[pltpu.VMEM((512, DEPTH), jnp.bfloat16)],
        compiler_params=pltpu.CompilerParams(vmem_limit_bytes=VMEM_BYTES),
    )(half, left, raised, near, far)


def body(eigenvectors, gauge_links, momenta):
    space = lax.axis_size("space")
    eig = lax.axis_size("eig")
    s = lax.axis_index("space")
    e = lax.axis_index("eig")
    block = eigenvectors.reshape(ROWS, DEPTH)
    row = lax.broadcasted_iota(jnp.int32, (5, 3), 0)
    column = lax.broadcasted_iota(jnp.int32, (5, 3), 1)
    plane = jnp.where(column == 0, s, space).astype(jnp.int32)
    plane = jnp.where(row < 4, jnp.pad(momenta, ((0, 1), (0, 0))), plane)
    half = (e & 1).astype(jnp.int32).reshape(1)
    groups = [list(range(0, eig, 2)), list(range(1, eig, 2))]

    partner = lax.ppermute(block, "eig", [(a, a ^ 1) for a in range(eig)])
    copies = jnp.broadcast_to(block[None], (eig // 2, ROWS, DEPTH))
    near = lax.all_to_all(
        copies, "eig", split_axis=0, concat_axis=0, axis_index_groups=groups, tiled=True
    ).reshape(eig // 2 * ROWS, DEPTH)
    left, raised = left_operand(plane, block, gauge_links)

    partner, left, raised = lax.optimization_barrier((partner, left, raised))
    raised = lax.ppermute(raised, "space", [(a, (a + 1) % space) for a in range(space)])
    partner, near = lax.optimization_barrier((partner, near))
    far = lax.all_gather(partner, "eig", axis_index_groups=groups, tiled=True)
    left, raised = left.reshape(8 * ROWS, DEPTH), raised.reshape(4 * ROWS, DEPTH)
    chunks = products(half, left, raised, near, far).reshape(space, 8, 12 * ROWS)
    got = lax.all_to_all(chunks, "space", split_axis=0, concat_axis=0, tiled=True)
    total = jnp.sum(got.astype(jnp.float32), axis=0)
    return total.reshape(2, 4, 3, 4, ROWS).transpose(2, 3, 0, 4, 1)


def solution(mesh):
    return jax.shard_map(
        body,
        mesh=mesh,
        in_specs=(
            P("eig", None, None, "space", None),
            P(None, None, None, None, "space", None),
            P(),
        ),
        out_specs=P(None, None, None, "eig", "space"),
        check_vma=False,
    )
```

```python
import math

import jax
import jax.numpy as jnp
from jax import lax
from jax.experimental import pallas as pl
from jax.experimental.pallas import tpu as pltpu
from jax.sharding import PartitionSpec as P

LX = 64
LY = 8
SITES = LX * LY
ROWS = 32
DEPTH = 6 * SITES
NEAR_ORDER = (1, 3, 0, 2)
VMEM_BYTES = 40 * 1024 * 1024


def moved_across(field):
    lane = lax.broadcasted_iota(jnp.int32, field.shape, 1)
    return jnp.where(
        lane % LX == 0, pltpu.roll(field, SITES - LX + 1, 1), pltpu.roll(field, 1, 1)
    )


def moved_along(field):
    return pltpu.roll(field, LX, 1)


MOVES = (moved_across, moved_along, lambda field: field)


def left_kernel(plane_ref, block_ref, link_ref, left_ref, raised_ref, table_ref):
    row = lax.broadcasted_iota(jnp.int32, (8, SITES), 0) % 4
    site = lax.broadcasted_iota(jnp.int32, (8, SITES), 1)

    def component(k):
        value = jnp.full((8, SITES), plane_ref[3, k], jnp.int32)
        for p in range(3):
            value = jnp.where(row == p, plane_ref[p, k], value)
        return value

    x_frac = ((component(0) * (site % LX)) & (LX - 1)).astype(jnp.float32) / LX
    y_frac = ((component(1) * (site // LX)) & (LY - 1)).astype(jnp.float32) / LY
    extent = plane_ref[4, 1]
    z_frac = ((component(2) * plane_ref[4, 0]) & (extent - 1)).astype(jnp.float32)
    z_frac = z_frac / extent.astype(jnp.float32)
    angles = 2.0 * math.pi * (x_frac + y_frac + z_frac)
    first = lax.broadcasted_iota(jnp.int32, (8, SITES), 0) < 4
    table = jnp.where(first, jnp.cos(angles), jnp.sin(angles))
    for d in range(3):
        table_ref[d] = MOVES[d](table)

    def rows_of(group, carry):
        rows = pl.ds(pl.multiple_of(group * 16, 16), 16)
        for d in range(3):
            for out_colour in range(3):
                real_base = jnp.zeros((16, SITES), jnp.float32)
                imag_base = jnp.zeros((16, SITES), jnp.float32)
                for colour in range(3):
                    at = 2 * SITES * colour
                    real_vec = block_ref[rows, at : at + SITES].astype(jnp.float32)
                    imag_vec = block_ref[rows, at + SITES : at + 2 * SITES].astype(jnp.float32)
                    real_link = link_ref[d, colour, out_colour, 0]
                    imag_link = link_ref[d, colour, out_colour, 1]
                    real_base += real_vec * real_link + imag_vec * imag_link
                    imag_base += real_vec * imag_link - imag_vec * real_link
                real_base, imag_base = MOVES[d](real_base), MOVES[d](imag_base)
                at = 2 * SITES * out_colour
                to_ref, to = (raised_ref, 0) if d == 2 else (left_ref, 4 * d)
                for p in range(4):
                    cosine = table_ref[d, p : p + 1, :]
                    sine = table_ref[d, p + 4 : p + 5, :]
                    to_ref[to + p, rows, at : at + SITES] = (
                        real_base * cosine + imag_base * sine
                    ).astype(jnp.bfloat16)
                    to_ref[to + p, rows, at + SITES : at + 2 * SITES] = (
                        imag_base * cosine - real_base * sine
                    ).astype(jnp.bfloat16)
        return carry

    lax.fori_loop(0, ROWS // 16, rows_of, 0)


def left_operand(plane, block, links):
    return pl.pallas_call(
        left_kernel,
        out_shape=[
            jax.ShapeDtypeStruct((8, ROWS, DEPTH), jnp.bfloat16),
            jax.ShapeDtypeStruct((4, ROWS, DEPTH), jnp.bfloat16),
        ],
        in_specs=[pl.BlockSpec(memory_space=pltpu.SMEM)]
        + [pl.BlockSpec(memory_space=pltpu.VMEM)] * 2,
        out_specs=[pl.BlockSpec(memory_space=pltpu.VMEM)] * 2,
        scratch_shapes=[pltpu.VMEM((3, 8, SITES), jnp.float32)],
        compiler_params=pltpu.CompilerParams(vmem_limit_bytes=VMEM_BYTES),
    )(plane, block, links)


def product_kernel(half_ref, left_ref, raised_ref, near_ref, far_ref, out_ref, both_ref):
    def spread(source_ref, to):
        real_rows, imag_rows = slice(to, to + 128), slice(to + 256, to + 384)
        for colour in range(3):
            at = 2 * SITES * colour
            real_vec = source_ref[:, at : at + SITES]
            imag_vec = source_ref[:, at + SITES : at + 2 * SITES]
            both_ref[real_rows, at : at + SITES] = real_vec
            both_ref[real_rows, at + SITES : at + 2 * SITES] = -imag_vec
            both_ref[imag_rows, at : at + SITES] = imag_vec
            both_ref[imag_rows, at + SITES : at + 2 * SITES] = real_vec

    def multiply(source_ref, least, most):
        product = lax.dot_general(
            both_ref[...],
            source_ref[...],
            (((1,), (1,)), ((), ())),
            preferred_element_type=jnp.float32,
        )
        width = most - least
        real_part = product[0:256].reshape(32, 8, width)
        imag_part = product[256:512].reshape(32, 8, width)
        upper = lax.broadcasted_iota(jnp.int32, (32, 8, width), 1) < 4
        even = jnp.where(upper, real_part, pltpu.roll(imag_part, 4, 1)).astype(jnp.bfloat16)
        odd = jnp.where(upper, pltpu.roll(real_part, 4, 1), imag_part).astype(jnp.bfloat16)
        for block in range(8):
            near = block < 4
            half = half_ref[0] if near else 1 - half_ref[0]
            place = NEAR_ORDER[block] if near else block - 4
            for pair in range(4):
                out_ref[place, half, 2 * pair, :, least:most] = even[4 * block + pair]
                out_ref[place, half, 2 * pair + 1, :, least:most] = odd[4 * block + pair]

    spread(near_ref, 0)
    spread(far_ref, 128)
    multiply(left_ref, 0, 8 * ROWS)
    multiply(raised_ref, 8 * ROWS, 12 * ROWS)


def products(half, left, raised, near, far):
    return pl.pallas_call(
        product_kernel,
        out_shape=jax.ShapeDtypeStruct((4, 2, 8, 8, 12 * ROWS), jnp.bfloat16),
        in_specs=[pl.BlockSpec(memory_space=pltpu.SMEM)]
        + [pl.BlockSpec(memory_space=pltpu.VMEM)] * 4,
        out_specs=pl.BlockSpec(memory_space=pltpu.VMEM),
        scratch_shapes=[pltpu.VMEM((512, DEPTH), jnp.bfloat16)],
        compiler_params=pltpu.CompilerParams(vmem_limit_bytes=VMEM_BYTES),
    )(half, left, raised, near, far)


def body(eigenvectors, gauge_links, momenta):
    space = lax.axis_size("space")
    eig = lax.axis_size("eig")
    s = lax.axis_index("space")
    e = lax.axis_index("eig")
    block = eigenvectors.reshape(ROWS, DEPTH)
    row = lax.broadcasted_iota(jnp.int32, (5, 3), 0)
    column = lax.broadcasted_iota(jnp.int32, (5, 3), 1)
    plane = jnp.where(column == 0, s, space).astype(jnp.int32)
    plane = jnp.where(row < 4, jnp.pad(momenta, ((0, 1), (0, 0))), plane)
    half = (e & 1).astype(jnp.int32).reshape(1)
    groups = [list(range(0, eig, 2)), list(range(1, eig, 2))]

    partner = lax.ppermute(block, "eig", [(a, a ^ 1) for a in range(eig)])
    copies = jnp.broadcast_to(block[None], (eig // 2, ROWS, DEPTH))
    near_groups = [[2 * x + h for x in NEAR_ORDER] for h in range(2)]
    near = lax.all_to_all(
        copies, "eig", split_axis=0, concat_axis=0, axis_index_groups=near_groups, tiled=True
    ).reshape(eig // 2 * ROWS, DEPTH)
    left, raised = left_operand(plane, block, gauge_links)

    partner, left, raised = lax.optimization_barrier((partner, left, raised))
    raised = lax.ppermute(raised, "space", [(a, (a + 1) % space) for a in range(space)])
    partner, near = lax.optimization_barrier((partner, near))
    far = lax.all_gather(partner, "eig", axis_index_groups=groups, tiled=True)
    left, raised = left.reshape(8 * ROWS, DEPTH), raised.reshape(4 * ROWS, DEPTH)
    chunks = products(half, left, raised, near, far).reshape(space, 8, 12 * ROWS)
    got = lax.all_to_all(chunks, "space", split_axis=0, concat_axis=0, tiled=True)
    total = jnp.sum(got.astype(jnp.float32), axis=0)
    return total.reshape(2, 4, 3, 4, ROWS).transpose(2, 3, 0, 4, 1)


def solution(mesh):
    return jax.shard_map(
        body,
        mesh=mesh,
        in_specs=(
            P("eig", None, None, "space", None),
            P(None, None, None, None, "space", None),
            P(),
        ),
        out_specs=P(None, None, None, "eig", "space"),
        check_vma=False,
    )
```

```python
import math

import jax
import jax.numpy as jnp
from jax import lax
from jax.experimental import pallas as pl
from jax.experimental.pallas import tpu as pltpu
from jax.sharding import PartitionSpec as P

LX = 64
LY = 8
SITES = LX * LY
ROWS = 32
DEPTH = 6 * SITES
NEAR_ORDER = (0, 1, 3, 2)
VMEM_BYTES = 40 * 1024 * 1024


def moved_across(field):
    lane = lax.broadcasted_iota(jnp.int32, field.shape, 1)
    return jnp.where(
        lane % LX == 0, pltpu.roll(field, SITES - LX + 1, 1), pltpu.roll(field, 1, 1)
    )


def moved_along(field):
    return pltpu.roll(field, LX, 1)


MOVES = (moved_across, moved_along, lambda field: field)


def left_kernel(plane_ref, block_ref, link_ref, left_ref, raised_ref, table_ref):
    row = lax.broadcasted_iota(jnp.int32, (8, SITES), 0) % 4
    site = lax.broadcasted_iota(jnp.int32, (8, SITES), 1)

    def component(k):
        value = jnp.full((8, SITES), plane_ref[3, k], jnp.int32)
        for p in range(3):
            value = jnp.where(row == p, plane_ref[p, k], value)
        return value

    x_frac = ((component(0) * (site % LX)) & (LX - 1)).astype(jnp.float32) / LX
    y_frac = ((component(1) * (site // LX)) & (LY - 1)).astype(jnp.float32) / LY
    extent = plane_ref[4, 1]
    z_frac = ((component(2) * plane_ref[4, 0]) & (extent - 1)).astype(jnp.float32)
    z_frac = z_frac / extent.astype(jnp.float32)
    angles = 2.0 * math.pi * (x_frac + y_frac + z_frac)
    first = lax.broadcasted_iota(jnp.int32, (8, SITES), 0) < 4
    table = jnp.where(first, jnp.cos(angles), jnp.sin(angles))
    for d in range(3):
        table_ref[d] = MOVES[d](table)

    def rows_of(group, carry):
        rows = pl.ds(pl.multiple_of(group * 16, 16), 16)
        for d in range(3):
            for out_colour in range(3):
                real_base = jnp.zeros((16, SITES), jnp.float32)
                imag_base = jnp.zeros((16, SITES), jnp.float32)
                for colour in range(3):
                    at = 2 * SITES * colour
                    real_vec = block_ref[rows, at : at + SITES].astype(jnp.float32)
                    imag_vec = block_ref[rows, at + SITES : at + 2 * SITES].astype(jnp.float32)
                    real_link = link_ref[d, colour, out_colour, 0]
                    imag_link = link_ref[d, colour, out_colour, 1]
                    real_base += real_vec * real_link + imag_vec * imag_link
                    imag_base += real_vec * imag_link - imag_vec * real_link
                real_base, imag_base = MOVES[d](real_base), MOVES[d](imag_base)
                at = 2 * SITES * out_colour
                to_ref, to = (raised_ref, 0) if d == 2 else (left_ref, 4 * d)
                for p in range(4):
                    cosine = table_ref[d, p : p + 1, :]
                    sine = table_ref[d, p + 4 : p + 5, :]
                    to_ref[to + p, rows, at : at + SITES] = (
                        real_base * cosine + imag_base * sine
                    ).astype(jnp.bfloat16)
                    to_ref[to + p, rows, at + SITES : at + 2 * SITES] = (
                        imag_base * cosine - real_base * sine
                    ).astype(jnp.bfloat16)
        return carry

    lax.fori_loop(0, ROWS // 16, rows_of, 0)


def left_operand(plane, block, links):
    return pl.pallas_call(
        left_kernel,
        out_shape=[
            jax.ShapeDtypeStruct((8, ROWS, DEPTH), jnp.bfloat16),
            jax.ShapeDtypeStruct((4, ROWS, DEPTH), jnp.bfloat16),
        ],
        in_specs=[pl.BlockSpec(memory_space=pltpu.SMEM)]
        + [pl.BlockSpec(memory_space=pltpu.VMEM)] * 2,
        out_specs=[pl.BlockSpec(memory_space=pltpu.VMEM)] * 2,
        scratch_shapes=[pltpu.VMEM((3, 8, SITES), jnp.float32)],
        compiler_params=pltpu.CompilerParams(vmem_limit_bytes=VMEM_BYTES),
    )(plane, block, links)


def product_kernel(half_ref, left_ref, raised_ref, near_ref, far_ref, out_ref, both_ref):
    def spread(source_ref, to):
        real_rows, imag_rows = slice(to, to + 128), slice(to + 256, to + 384)
        for colour in range(3):
            at = 2 * SITES * colour
            real_vec = source_ref[:, at : at + SITES]
            imag_vec = source_ref[:, at + SITES : at + 2 * SITES]
            both_ref[real_rows, at : at + SITES] = real_vec
            both_ref[real_rows, at + SITES : at + 2 * SITES] = -imag_vec
            both_ref[imag_rows, at : at + SITES] = imag_vec
            both_ref[imag_rows, at + SITES : at + 2 * SITES] = real_vec

    def multiply(source_ref, least, most):
        product = lax.dot_general(
            both_ref[...],
            source_ref[...],
            (((1,), (1,)), ((), ())),
            preferred_element_type=jnp.float32,
        )
        width = most - least
        real_part = product[0:256].reshape(32, 8, width)
        imag_part = product[256:512].reshape(32, 8, width)
        upper = lax.broadcasted_iota(jnp.int32, (32, 8, width), 1) < 4
        even = jnp.where(upper, real_part, pltpu.roll(imag_part, 4, 1)).astype(jnp.bfloat16)
        odd = jnp.where(upper, pltpu.roll(real_part, 4, 1), imag_part).astype(jnp.bfloat16)
        for block in range(8):
            near = block < 4
            half = half_ref[0] if near else 1 - half_ref[0]
            place = NEAR_ORDER[block] if near else block - 4
            for pair in range(4):
                out_ref[place, half, 2 * pair, :, least:most] = even[4 * block + pair]
                out_ref[place, half, 2 * pair + 1, :, least:most] = odd[4 * block + pair]

    spread(near_ref, 0)
    spread(far_ref, 128)
    multiply(left_ref, 0, 8 * ROWS)
    multiply(raised_ref, 8 * ROWS, 12 * ROWS)


def products(half, left, raised, near, far):
    return pl.pallas_call(
        product_kernel,
        out_shape=jax.ShapeDtypeStruct((4, 2, 8, 8, 12 * ROWS), jnp.bfloat16),
        in_specs=[pl.BlockSpec(memory_space=pltpu.SMEM)]
        + [pl.BlockSpec(memory_space=pltpu.VMEM)] * 4,
        out_specs=pl.BlockSpec(memory_space=pltpu.VMEM),
        scratch_shapes=[pltpu.VMEM((512, DEPTH), jnp.bfloat16)],
        compiler_params=pltpu.CompilerParams(vmem_limit_bytes=VMEM_BYTES),
    )(half, left, raised, near, far)


def body(eigenvectors, gauge_links, momenta):
    space = lax.axis_size("space")
    eig = lax.axis_size("eig")
    s = lax.axis_index("space")
    e = lax.axis_index("eig")
    block = eigenvectors.reshape(ROWS, DEPTH)
    row = lax.broadcasted_iota(jnp.int32, (5, 3), 0)
    column = lax.broadcasted_iota(jnp.int32, (5, 3), 1)
    plane = jnp.where(column == 0, s, space).astype(jnp.int32)
    plane = jnp.where(row < 4, jnp.pad(momenta, ((0, 1), (0, 0))), plane)
    half = (e & 1).astype(jnp.int32).reshape(1)
    groups = [list(range(0, eig, 2)), list(range(1, eig, 2))]

    partner = lax.ppermute(block, "eig", [(a, a ^ 1) for a in range(eig)])
    copies = jnp.broadcast_to(block[None], (eig // 2, ROWS, DEPTH))
    near_groups = [[2 * x + h for x in NEAR_ORDER] for h in range(2)]
    near = lax.all_to_all(
        copies, "eig", split_axis=0, concat_axis=0, axis_index_groups=near_groups, tiled=True
    ).reshape(eig // 2 * ROWS, DEPTH)
    left, raised = left_operand(plane, block, gauge_links)

    partner, left, raised = lax.optimization_barrier((partner, left, raised))
    raised = lax.ppermute(raised, "space", [(a, (a + 1) % space) for a in range(space)])
    partner, near = lax.optimization_barrier((partner, near))
    far = lax.all_gather(partner, "eig", axis_index_groups=groups, tiled=True)
    left, raised = left.reshape(8 * ROWS, DEPTH), raised.reshape(4 * ROWS, DEPTH)
    chunks = products(half, left, raised, near, far).reshape(space, 8, 12 * ROWS)
    got = lax.all_to_all(chunks, "space", split_axis=0, concat_axis=0, tiled=True)
    total = jnp.sum(got.astype(jnp.float32), axis=0)
    return total.reshape(2, 4, 3, 4, ROWS).transpose(2, 3, 0, 4, 1)


def solution(mesh):
    return jax.shard_map(
        body,
        mesh=mesh,
        in_specs=(
            P("eig", None, None, "space", None),
            P(None, None, None, None, "space", None),
            P(),
        ),
        out_specs=P(None, None, None, "eig", "space"),
        check_vma=False,
    )
```

```python
import math

import jax
import jax.numpy as jnp
from jax import lax
from jax.experimental import pallas as pl
from jax.experimental.pallas import tpu as pltpu
from jax.sharding import PartitionSpec as P

LX = 64
LY = 8
SITES = LX * LY
ROWS = 32
DEPTH = 6 * SITES
PAD = 1024
NEAR_ORDER = (1, 3, 0, 2)
VMEM_BYTES = 40 * 1024 * 1024


def moved_across(field):
    lane = lax.broadcasted_iota(jnp.int32, field.shape, 1)
    return jnp.where(
        lane % LX == 0, pltpu.roll(field, SITES - LX + 1, 1), pltpu.roll(field, 1, 1)
    )


def moved_along(field):
    return pltpu.roll(field, LX, 1)


MOVES = (moved_across, moved_along, lambda field: field)


def left_kernel(plane_ref, block_ref, link_ref, left_ref, raised_ref, table_ref):
    row = lax.broadcasted_iota(jnp.int32, (8, SITES), 0) % 4
    site = lax.broadcasted_iota(jnp.int32, (8, SITES), 1)

    def component(k):
        value = jnp.full((8, SITES), plane_ref[3, k], jnp.int32)
        for p in range(3):
            value = jnp.where(row == p, plane_ref[p, k], value)
        return value

    x_frac = ((component(0) * (site % LX)) & (LX - 1)).astype(jnp.float32) / LX
    y_frac = ((component(1) * (site // LX)) & (LY - 1)).astype(jnp.float32) / LY
    extent = plane_ref[4, 1]
    z_frac = ((component(2) * plane_ref[4, 0]) & (extent - 1)).astype(jnp.float32)
    z_frac = z_frac / extent.astype(jnp.float32)
    angles = 2.0 * math.pi * (x_frac + y_frac + z_frac)
    first = lax.broadcasted_iota(jnp.int32, (8, SITES), 0) < 4
    table = jnp.where(first, jnp.cos(angles), jnp.sin(angles))
    for d in range(3):
        table_ref[d] = MOVES[d](table)

    def rows_of(group, carry):
        rows = pl.ds(pl.multiple_of(group * 16, 16), 16)
        for d in range(3):
            for out_colour in range(3):
                real_base = jnp.zeros((16, SITES), jnp.float32)
                imag_base = jnp.zeros((16, SITES), jnp.float32)
                for colour in range(3):
                    at = 2 * SITES * colour
                    real_vec = block_ref[rows, at : at + SITES].astype(jnp.float32)
                    imag_vec = block_ref[rows, at + SITES : at + 2 * SITES].astype(jnp.float32)
                    real_link = link_ref[d, colour, out_colour, 0]
                    imag_link = link_ref[d, colour, out_colour, 1]
                    real_base += real_vec * real_link + imag_vec * imag_link
                    imag_base += real_vec * imag_link - imag_vec * real_link
                real_base, imag_base = MOVES[d](real_base), MOVES[d](imag_base)
                at = 2 * SITES * out_colour
                to_ref, to = (raised_ref, 0) if d == 2 else (left_ref, 4 * d)
                for p in range(4):
                    cosine = table_ref[d, p : p + 1, :]
                    sine = table_ref[d, p + 4 : p + 5, :]
                    to_ref[to + p, rows, at : at + SITES] = (
                        real_base * cosine + imag_base * sine
                    ).astype(jnp.bfloat16)
                    to_ref[to + p, rows, at + SITES : at + 2 * SITES] = (
                        imag_base * cosine - real_base * sine
                    ).astype(jnp.bfloat16)
        return carry

    lax.fori_loop(0, ROWS // 16, rows_of, 0)


def left_operand(plane, block, links):
    return pl.pallas_call(
        left_kernel,
        out_shape=[
            jax.ShapeDtypeStruct((8, ROWS, DEPTH), jnp.bfloat16),
            jax.ShapeDtypeStruct((4, ROWS, DEPTH), jnp.bfloat16),
        ],
        in_specs=[pl.BlockSpec(memory_space=pltpu.SMEM)]
        + [pl.BlockSpec(memory_space=pltpu.VMEM)] * 2,
        out_specs=[pl.BlockSpec(memory_space=pltpu.VMEM)] * 2,
        scratch_shapes=[pltpu.VMEM((3, 8, SITES), jnp.float32)],
        compiler_params=pltpu.CompilerParams(vmem_limit_bytes=VMEM_BYTES),
    )(plane, block, links)


def product_kernel(half_ref, left_ref, raised_ref, near_ref, far_ref, out_ref, both_ref):
    def spread(source_ref, to):
        real_rows, imag_rows = slice(to, to + 128), slice(to + 256, to + 384)
        for colour in range(3):
            at = 2 * SITES * colour
            real_vec = source_ref[:, at : at + SITES]
            imag_vec = source_ref[:, at + SITES : at + 2 * SITES]
            both_ref[real_rows, at : at + SITES] = real_vec
            both_ref[real_rows, at + SITES : at + 2 * SITES] = -imag_vec
            both_ref[imag_rows, at : at + SITES] = imag_vec
            both_ref[imag_rows, at + SITES : at + 2 * SITES] = real_vec

    def multiply(source_ref, least, most):
        product = lax.dot_general(
            both_ref[...],
            source_ref[...],
            (((1,), (1,)), ((), ())),
            preferred_element_type=jnp.float32,
        )
        width = most - least
        real_part = product[0:256].reshape(32, 8, width)
        imag_part = product[256:512].reshape(32, 8, width)
        upper = lax.broadcasted_iota(jnp.int32, (32, 8, width), 1) < 4
        even = jnp.where(upper, real_part, pltpu.roll(imag_part, 4, 1)).astype(jnp.bfloat16)
        odd = jnp.where(upper, pltpu.roll(real_part, 4, 1), imag_part).astype(jnp.bfloat16)
        for block in range(8):
            near = block < 4
            half = half_ref[0] if near else 1 - half_ref[0]
            place = NEAR_ORDER[block] if near else block - 4
            for pair in range(4):
                out_ref[place, half, 2 * pair, :, least:most] = even[4 * block + pair]
                out_ref[place, half, 2 * pair + 1, :, least:most] = odd[4 * block + pair]

    spread(near_ref, 0)
    spread(far_ref, 128)
    multiply(left_ref, 0, 8 * ROWS)
    multiply(raised_ref, 8 * ROWS, 12 * ROWS)


def products(half, left, raised, near, far):
    return pl.pallas_call(
        product_kernel,
        out_shape=jax.ShapeDtypeStruct((4, 2, 8, 8, 12 * ROWS), jnp.bfloat16),
        in_specs=[pl.BlockSpec(memory_space=pltpu.SMEM)]
        + [pl.BlockSpec(memory_space=pltpu.VMEM)] * 4,
        out_specs=pl.BlockSpec(memory_space=pltpu.VMEM),
        scratch_shapes=[pltpu.VMEM((512, DEPTH), jnp.bfloat16)],
        compiler_params=pltpu.CompilerParams(vmem_limit_bytes=VMEM_BYTES),
    )(half, left, raised, near, far)


def body(eigenvectors, gauge_links, momenta):
    space = lax.axis_size("space")
    eig = lax.axis_size("eig")
    s = lax.axis_index("space")
    e = lax.axis_index("eig")
    block = eigenvectors.reshape(ROWS, DEPTH)
    row = lax.broadcasted_iota(jnp.int32, (5, 3), 0)
    column = lax.broadcasted_iota(jnp.int32, (5, 3), 1)
    plane = jnp.where(column == 0, s, space).astype(jnp.int32)
    plane = jnp.where(row < 4, jnp.pad(momenta, ((0, 1), (0, 0))), plane)
    half = (e & 1).astype(jnp.int32).reshape(1)
    groups = [list(range(0, eig, 2)), list(range(1, eig, 2))]

    partner = lax.ppermute(block, "eig", [(a, a ^ 1) for a in range(eig)])
    copies = jnp.pad(block, ((0, 0), (0, PAD)))
    copies = jnp.broadcast_to(copies[None], (eig // 2, ROWS, DEPTH + PAD))
    near_groups = [[2 * x + h for x in NEAR_ORDER] for h in range(2)]
    near = lax.all_to_all(
        copies, "eig", split_axis=0, concat_axis=0, axis_index_groups=near_groups, tiled=True
    ).reshape(eig // 2 * ROWS, DEPTH + PAD)
    left, raised = left_operand(plane, block, gauge_links)

    partner, left, raised = lax.optimization_barrier((partner, left, raised))
    raised = lax.ppermute(raised, "space", [(a, (a + 1) % space) for a in range(space)])
    far = lax.all_gather(partner, "eig", axis_index_groups=groups, tiled=True)
    left, raised = left.reshape(8 * ROWS, DEPTH), raised.reshape(4 * ROWS, DEPTH)
    chunks = products(half, left, raised, near, far).reshape(space, 8, 12 * ROWS)
    got = lax.all_to_all(chunks, "space", split_axis=0, concat_axis=0, tiled=True)
    total = jnp.sum(got.astype(jnp.float32), axis=0)
    return total.reshape(2, 4, 3, 4, ROWS).transpose(2, 3, 0, 4, 1)


def solution(mesh):
    return jax.shard_map(
        body,
        mesh=mesh,
        in_specs=(
            P("eig", None, None, "space", None),
            P(None, None, None, None, "space", None),
            P(),
        ),
        out_specs=P(None, None, None, "eig", "space"),
        check_vma=False,
    )
```

```python
import math

import jax
import jax.numpy as jnp
from jax import lax
from jax.experimental import pallas as pl
from jax.experimental.pallas import tpu as pltpu
from jax.sharding import PartitionSpec as P

LX = 64
LY = 8
SITES = LX * LY
ROWS = 32
DEPTH = 6 * SITES
PAD = 1024
NEAR_ORDER = (1, 3, 0, 2)
VMEM_BYTES = 40 * 1024 * 1024


def moved_across(field):
    lane = lax.broadcasted_iota(jnp.int32, field.shape, 1)
    return jnp.where(
        lane % LX == 0, pltpu.roll(field, SITES - LX + 1, 1), pltpu.roll(field, 1, 1)
    )


def moved_along(field):
    return pltpu.roll(field, LX, 1)


MOVES = (moved_across, moved_along, lambda field: field)


def left_kernel(plane_ref, block_ref, link_ref, left_ref, raised_ref, table_ref):
    row = lax.broadcasted_iota(jnp.int32, (8, SITES), 0) % 4
    site = lax.broadcasted_iota(jnp.int32, (8, SITES), 1)

    def component(k):
        value = jnp.full((8, SITES), plane_ref[3, k], jnp.int32)
        for p in range(3):
            value = jnp.where(row == p, plane_ref[p, k], value)
        return value

    x_frac = ((component(0) * (site % LX)) & (LX - 1)).astype(jnp.float32) / LX
    y_frac = ((component(1) * (site // LX)) & (LY - 1)).astype(jnp.float32) / LY
    extent = plane_ref[4, 1]
    z_frac = ((component(2) * plane_ref[4, 0]) & (extent - 1)).astype(jnp.float32)
    z_frac = z_frac / extent.astype(jnp.float32)
    angles = 2.0 * math.pi * (x_frac + y_frac + z_frac)
    first = lax.broadcasted_iota(jnp.int32, (8, SITES), 0) < 4
    table = jnp.where(first, jnp.cos(angles), jnp.sin(angles))
    for d in range(3):
        table_ref[d] = MOVES[d](table)

    def rows_of(group, carry):
        rows = pl.ds(pl.multiple_of(group * 16, 16), 16)
        for d in range(3):
            for out_colour in range(3):
                real_base = jnp.zeros((16, SITES), jnp.float32)
                imag_base = jnp.zeros((16, SITES), jnp.float32)
                for colour in range(3):
                    at = 2 * SITES * colour
                    real_vec = block_ref[rows, at : at + SITES].astype(jnp.float32)
                    imag_vec = block_ref[rows, at + SITES : at + 2 * SITES].astype(jnp.float32)
                    real_link = link_ref[d, colour, out_colour, 0]
                    imag_link = link_ref[d, colour, out_colour, 1]
                    real_base += real_vec * real_link + imag_vec * imag_link
                    imag_base += real_vec * imag_link - imag_vec * real_link
                real_base, imag_base = MOVES[d](real_base), MOVES[d](imag_base)
                at = 2 * SITES * out_colour
                to_ref, to = (raised_ref, 0) if d == 2 else (left_ref, 4 * d)
                for p in range(4):
                    cosine = table_ref[d, p : p + 1, :]
                    sine = table_ref[d, p + 4 : p + 5, :]
                    to_ref[to + p, rows, at : at + SITES] = (
                        real_base * cosine + imag_base * sine
                    ).astype(jnp.bfloat16)
                    to_ref[to + p, rows, at + SITES : at + 2 * SITES] = (
                        imag_base * cosine - real_base * sine
                    ).astype(jnp.bfloat16)
        return carry

    lax.fori_loop(0, ROWS // 16, rows_of, 0)


def left_operand(plane, block, links):
    return pl.pallas_call(
        left_kernel,
        out_shape=[
            jax.ShapeDtypeStruct((8, ROWS, DEPTH), jnp.bfloat16),
            jax.ShapeDtypeStruct((4, ROWS, DEPTH), jnp.bfloat16),
        ],
        in_specs=[pl.BlockSpec(memory_space=pltpu.SMEM)]
        + [pl.BlockSpec(memory_space=pltpu.VMEM)] * 2,
        out_specs=[pl.BlockSpec(memory_space=pltpu.VMEM)] * 2,
        scratch_shapes=[pltpu.VMEM((3, 8, SITES), jnp.float32)],
        compiler_params=pltpu.CompilerParams(vmem_limit_bytes=VMEM_BYTES),
    )(plane, block, links)


def product_kernel(
    half_ref, left_ref, raised_in, near_ref, far_ref, out_ref, both_ref, raised_ref, raised_sem
):
    raised_copy = pltpu.make_async_copy(raised_in, raised_ref, raised_sem)
    raised_copy.start()

    def spread(source_ref, to):
        real_rows, imag_rows = slice(to, to + 128), slice(to + 256, to + 384)
        for colour in range(3):
            at = 2 * SITES * colour
            real_vec = source_ref[:, at : at + SITES]
            imag_vec = source_ref[:, at + SITES : at + 2 * SITES]
            both_ref[real_rows, at : at + SITES] = real_vec
            both_ref[real_rows, at + SITES : at + 2 * SITES] = -imag_vec
            both_ref[imag_rows, at : at + SITES] = imag_vec
            both_ref[imag_rows, at + SITES : at + 2 * SITES] = real_vec

    def multiply(source_ref, least, most):
        product = lax.dot_general(
            both_ref[...],
            source_ref[...],
            (((1,), (1,)), ((), ())),
            preferred_element_type=jnp.float32,
        )
        width = most - least
        real_part = product[0:256].reshape(32, 8, width)
        imag_part = product[256:512].reshape(32, 8, width)
        upper = lax.broadcasted_iota(jnp.int32, (32, 8, width), 1) < 4
        even = jnp.where(upper, real_part, pltpu.roll(imag_part, 4, 1)).astype(jnp.bfloat16)
        odd = jnp.where(upper, pltpu.roll(real_part, 4, 1), imag_part).astype(jnp.bfloat16)
        for block in range(8):
            near = block < 4
            half = half_ref[0] if near else 1 - half_ref[0]
            place = NEAR_ORDER[block] if near else block - 4
            for pair in range(4):
                out_ref[place, half, 2 * pair, :, least:most] = even[4 * block + pair]
                out_ref[place, half, 2 * pair + 1, :, least:most] = odd[4 * block + pair]

    spread(near_ref, 0)
    spread(far_ref, 128)
    multiply(left_ref, 0, 8 * ROWS)
    raised_copy.wait()
    multiply(raised_ref, 8 * ROWS, 12 * ROWS)


def products(half, left, raised, near, far):
    return pl.pallas_call(
        product_kernel,
        out_shape=jax.ShapeDtypeStruct((4, 2, 8, 8, 12 * ROWS), jnp.bfloat16),
        in_specs=[
            pl.BlockSpec(memory_space=pltpu.SMEM),
            pl.BlockSpec(memory_space=pltpu.VMEM),
            pl.BlockSpec(memory_space=pl.ANY),
            pl.BlockSpec(memory_space=pltpu.VMEM),
            pl.BlockSpec(memory_space=pltpu.VMEM),
        ],
        out_specs=pl.BlockSpec(memory_space=pltpu.VMEM),
        scratch_shapes=[
            pltpu.VMEM((512, DEPTH), jnp.bfloat16),
            pltpu.VMEM((4 * ROWS, DEPTH), jnp.bfloat16),
            pltpu.SemaphoreType.DMA,
        ],
        compiler_params=pltpu.CompilerParams(vmem_limit_bytes=VMEM_BYTES),
    )(half, left, raised, near, far)


def body(eigenvectors, gauge_links, momenta):
    space = lax.axis_size("space")
    eig = lax.axis_size("eig")
    s = lax.axis_index("space")
    e = lax.axis_index("eig")
    block = eigenvectors.reshape(ROWS, DEPTH)
    row = lax.broadcasted_iota(jnp.int32, (5, 3), 0)
    column = lax.broadcasted_iota(jnp.int32, (5, 3), 1)
    plane = jnp.where(column == 0, s, space).astype(jnp.int32)
    plane = jnp.where(row < 4, jnp.pad(momenta, ((0, 1), (0, 0))), plane)
    half = (e & 1).astype(jnp.int32).reshape(1)
    groups = [list(range(0, eig, 2)), list(range(1, eig, 2))]

    partner = lax.ppermute(block, "eig", [(a, a ^ 1) for a in range(eig)])
    copies = jnp.pad(block, ((0, 0), (0, PAD)))
    copies = jnp.broadcast_to(copies[None], (eig // 2, ROWS, DEPTH + PAD))
    near_groups = [[2 * x + h for x in NEAR_ORDER] for h in range(2)]
    near = lax.all_to_all(
        copies, "eig", split_axis=0, concat_axis=0, axis_index_groups=near_groups, tiled=True
    ).reshape(eig // 2 * ROWS, DEPTH + PAD)
    left, raised = left_operand(plane, block, gauge_links)

    partner, left, raised = lax.optimization_barrier((partner, left, raised))
    raised = lax.ppermute(raised, "space", [(a, (a + 1) % space) for a in range(space)])
    far = lax.all_gather(partner, "eig", axis_index_groups=groups, tiled=True)
    left, raised = left.reshape(8 * ROWS, DEPTH), raised.reshape(4 * ROWS, DEPTH)
    chunks = products(half, left, raised, near, far).reshape(space, 8, 12 * ROWS)
    got = lax.all_to_all(chunks, "space", split_axis=0, concat_axis=0, tiled=True)
    total = jnp.sum(got.astype(jnp.float32), axis=0)
    return total.reshape(2, 4, 3, 4, ROWS).transpose(2, 3, 0, 4, 1)


def solution(mesh):
    return jax.shard_map(
        body,
        mesh=mesh,
        in_specs=(
            P("eig", None, None, "space", None),
            P(None, None, None, None, "space", None),
            P(),
        ),
        out_specs=P(None, None, None, "eig", "space"),
        check_vma=False,
    )
```

```python
import math

import jax
import jax.numpy as jnp
from jax import lax
from jax.experimental import pallas as pl
from jax.experimental.pallas import tpu as pltpu
from jax.sharding import PartitionSpec as P

LX = 64
LY = 8
SITES = LX * LY
ROWS = 32
DEPTH = 6 * SITES
PAD = 1024
NEAR_ORDER = (1, 3, 0, 2)
VMEM_BYTES = 40 * 1024 * 1024


def moved_across(field):
    lane = lax.broadcasted_iota(jnp.int32, field.shape, 1)
    return jnp.where(
        lane % LX == 0, pltpu.roll(field, SITES - LX + 1, 1), pltpu.roll(field, 1, 1)
    )


def moved_along(field):
    return pltpu.roll(field, LX, 1)


MOVES = (moved_across, moved_along, lambda field: field)


def left_kernel(plane_ref, block_ref, link_ref, left_ref, raised_ref, table_ref):
    row = lax.broadcasted_iota(jnp.int32, (8, SITES), 0) % 4
    site = lax.broadcasted_iota(jnp.int32, (8, SITES), 1)

    def component(k):
        value = jnp.full((8, SITES), plane_ref[3, k], jnp.int32)
        for p in range(3):
            value = jnp.where(row == p, plane_ref[p, k], value)
        return value

    x_frac = ((component(0) * (site % LX)) & (LX - 1)).astype(jnp.float32) / LX
    y_frac = ((component(1) * (site // LX)) & (LY - 1)).astype(jnp.float32) / LY
    extent = plane_ref[4, 1]
    z_frac = ((component(2) * plane_ref[4, 0]) & (extent - 1)).astype(jnp.float32)
    z_frac = z_frac / extent.astype(jnp.float32)
    angles = 2.0 * math.pi * (x_frac + y_frac + z_frac)
    first = lax.broadcasted_iota(jnp.int32, (8, SITES), 0) < 4
    table = jnp.where(first, jnp.cos(angles), jnp.sin(angles))
    for d in range(3):
        table_ref[d] = MOVES[d](table)

    def rows_of(group, carry):
        rows = pl.ds(pl.multiple_of(group * 16, 16), 16)
        for d in range(3):
            for out_colour in range(3):
                real_base = jnp.zeros((16, SITES), jnp.float32)
                imag_base = jnp.zeros((16, SITES), jnp.float32)
                for colour in range(3):
                    at = 2 * SITES * colour
                    real_vec = block_ref[rows, at : at + SITES].astype(jnp.float32)
                    imag_vec = block_ref[rows, at + SITES : at + 2 * SITES].astype(jnp.float32)
                    real_link = link_ref[d, colour, out_colour, 0]
                    imag_link = link_ref[d, colour, out_colour, 1]
                    real_base += real_vec * real_link + imag_vec * imag_link
                    imag_base += real_vec * imag_link - imag_vec * real_link
                real_base, imag_base = MOVES[d](real_base), MOVES[d](imag_base)
                at = 2 * SITES * out_colour
                to_ref, to = (raised_ref, 0) if d == 2 else (left_ref, 4 * d)
                for p in range(4):
                    cosine = table_ref[d, p : p + 1, :]
                    sine = table_ref[d, p + 4 : p + 5, :]
                    to_ref[to + p, rows, at : at + SITES] = (
                        real_base * cosine + imag_base * sine
                    ).astype(jnp.bfloat16)
                    to_ref[to + p, rows, at + SITES : at + 2 * SITES] = (
                        imag_base * cosine - real_base * sine
                    ).astype(jnp.bfloat16)
        return carry

    lax.fori_loop(0, ROWS // 16, rows_of, 0)


def left_operand(plane, block, links):
    return pl.pallas_call(
        left_kernel,
        out_shape=[
            jax.ShapeDtypeStruct((8, ROWS, DEPTH), jnp.bfloat16),
            jax.ShapeDtypeStruct((4, ROWS, DEPTH), jnp.bfloat16),
        ],
        in_specs=[pl.BlockSpec(memory_space=pltpu.SMEM)]
        + [pl.BlockSpec(memory_space=pltpu.VMEM)] * 2,
        out_specs=[pl.BlockSpec(memory_space=pltpu.VMEM)] * 2,
        scratch_shapes=[pltpu.VMEM((3, 8, SITES), jnp.float32)],
        compiler_params=pltpu.CompilerParams(vmem_limit_bytes=VMEM_BYTES),
    )(plane, block, links)


def product_kernel(
    half_ref, left_ref, raised_in, near_ref, far_ref, out_ref, both_ref, raised_ref, raised_sem
):
    copies = []
    for piece in range(8):
        rows = pl.ds(16 * piece, 16)
        copies.append(
            pltpu.make_async_copy(raised_in.at[rows], raised_ref.at[rows], raised_sem.at[piece])
        )
        copies[piece].start()

    def spread(source_ref, to):
        real_rows, imag_rows = slice(to, to + 128), slice(to + 256, to + 384)
        for colour in range(3):
            at = 2 * SITES * colour
            real_vec = source_ref[:, at : at + SITES]
            imag_vec = source_ref[:, at + SITES : at + 2 * SITES]
            both_ref[real_rows, at : at + SITES] = real_vec
            both_ref[real_rows, at + SITES : at + 2 * SITES] = -imag_vec
            both_ref[imag_rows, at : at + SITES] = imag_vec
            both_ref[imag_rows, at + SITES : at + 2 * SITES] = real_vec

    def multiply(source_ref, least, most):
        product = lax.dot_general(
            both_ref[...],
            source_ref[...],
            (((1,), (1,)), ((), ())),
            preferred_element_type=jnp.float32,
        )
        width = most - least
        real_part = product[0:256].reshape(32, 8, width)
        imag_part = product[256:512].reshape(32, 8, width)
        upper = lax.broadcasted_iota(jnp.int32, (32, 8, width), 1) < 4
        even = jnp.where(upper, real_part, pltpu.roll(imag_part, 4, 1)).astype(jnp.bfloat16)
        odd = jnp.where(upper, pltpu.roll(real_part, 4, 1), imag_part).astype(jnp.bfloat16)
        for block in range(8):
            near = block < 4
            half = half_ref[0] if near else 1 - half_ref[0]
            place = NEAR_ORDER[block] if near else block - 4
            for pair in range(4):
                out_ref[place, half, 2 * pair, :, least:most] = even[4 * block + pair]
                out_ref[place, half, 2 * pair + 1, :, least:most] = odd[4 * block + pair]

    spread(near_ref, 0)
    spread(far_ref, 128)
    multiply(left_ref, 0, 8 * ROWS)
    for copy in copies:
        copy.wait()
    multiply(raised_ref, 8 * ROWS, 12 * ROWS)


def products(half, left, raised, near, far):
    return pl.pallas_call(
        product_kernel,
        out_shape=jax.ShapeDtypeStruct((4, 2, 8, 8, 12 * ROWS), jnp.bfloat16),
        in_specs=[
            pl.BlockSpec(memory_space=pltpu.SMEM),
            pl.BlockSpec(memory_space=pltpu.VMEM),
            pl.BlockSpec(memory_space=pl.ANY),
            pl.BlockSpec(memory_space=pltpu.VMEM),
            pl.BlockSpec(memory_space=pltpu.VMEM),
        ],
        out_specs=pl.BlockSpec(memory_space=pltpu.VMEM),
        scratch_shapes=[
            pltpu.VMEM((512, DEPTH), jnp.bfloat16),
            pltpu.VMEM((4 * ROWS, DEPTH), jnp.bfloat16),
            pltpu.SemaphoreType.DMA((8,)),
        ],
        compiler_params=pltpu.CompilerParams(vmem_limit_bytes=VMEM_BYTES),
    )(half, left, raised, near, far)


def body(eigenvectors, gauge_links, momenta):
    space = lax.axis_size("space")
    eig = lax.axis_size("eig")
    s = lax.axis_index("space")
    e = lax.axis_index("eig")
    block = eigenvectors.reshape(ROWS, DEPTH)
    row = lax.broadcasted_iota(jnp.int32, (5, 3), 0)
    column = lax.broadcasted_iota(jnp.int32, (5, 3), 1)
    plane = jnp.where(column == 0, s, space).astype(jnp.int32)
    plane = jnp.where(row < 4, jnp.pad(momenta, ((0, 1), (0, 0))), plane)
    half = (e & 1).astype(jnp.int32).reshape(1)
    groups = [list(range(0, eig, 2)), list(range(1, eig, 2))]

    partner = lax.ppermute(block, "eig", [(a, a ^ 1) for a in range(eig)])
    copies = jnp.pad(block, ((0, 0), (0, PAD)))
    copies = jnp.broadcast_to(copies[None], (eig // 2, ROWS, DEPTH + PAD))
    near_groups = [[2 * x + h for x in NEAR_ORDER] for h in range(2)]
    near = lax.all_to_all(
        copies, "eig", split_axis=0, concat_axis=0, axis_index_groups=near_groups, tiled=True
    ).reshape(eig // 2 * ROWS, DEPTH + PAD)
    left, raised = left_operand(plane, block, gauge_links)

    partner, left, raised = lax.optimization_barrier((partner, left, raised))
    raised = lax.ppermute(raised, "space", [(a, (a + 1) % space) for a in range(space)])
    far = lax.all_gather(partner, "eig", axis_index_groups=groups, tiled=True)
    left, raised = left.reshape(8 * ROWS, DEPTH), raised.reshape(4 * ROWS, DEPTH)
    chunks = products(half, left, raised, near, far).reshape(space, 8, 12 * ROWS)
    got = lax.all_to_all(chunks, "space", split_axis=0, concat_axis=0, tiled=True)
    total = jnp.sum(got.astype(jnp.float32), axis=0)
    return total.reshape(2, 4, 3, 4, ROWS).transpose(2, 3, 0, 4, 1)


def solution(mesh):
    return jax.shard_map(
        body,
        mesh=mesh,
        in_specs=(
            P("eig", None, None, "space", None),
            P(None, None, None, None, "space", None),
            P(),
        ),
        out_specs=P(None, None, None, "eig", "space"),
        check_vma=False,
    )
```

```python
import math

import jax
import jax.numpy as jnp
from jax import lax
from jax.experimental import pallas as pl
from jax.experimental.pallas import tpu as pltpu
from jax.sharding import PartitionSpec as P

LX = 64
LY = 8
SITES = LX * LY
ROWS = 32
DEPTH = 6 * SITES
PAD = 1024
NEAR_ORDER = (0, 1, 2, 3)
VMEM_BYTES = 40 * 1024 * 1024


def moved_across(field):
    lane = lax.broadcasted_iota(jnp.int32, field.shape, 1)
    return jnp.where(
        lane % LX == 0, pltpu.roll(field, SITES - LX + 1, 1), pltpu.roll(field, 1, 1)
    )


def moved_along(field):
    return pltpu.roll(field, LX, 1)


MOVES = (moved_across, moved_along, lambda field: field)


def left_kernel(plane_ref, block_ref, link_ref, left_ref, raised_ref, table_ref):
    row = lax.broadcasted_iota(jnp.int32, (8, SITES), 0) % 4
    site = lax.broadcasted_iota(jnp.int32, (8, SITES), 1)

    def component(k):
        value = jnp.full((8, SITES), plane_ref[3, k], jnp.int32)
        for p in range(3):
            value = jnp.where(row == p, plane_ref[p, k], value)
        return value

    x_frac = ((component(0) * (site % LX)) & (LX - 1)).astype(jnp.float32) / LX
    y_frac = ((component(1) * (site // LX)) & (LY - 1)).astype(jnp.float32) / LY
    extent = plane_ref[4, 1]
    z_frac = ((component(2) * plane_ref[4, 0]) & (extent - 1)).astype(jnp.float32)
    z_frac = z_frac / extent.astype(jnp.float32)
    angles = 2.0 * math.pi * (x_frac + y_frac + z_frac)
    first = lax.broadcasted_iota(jnp.int32, (8, SITES), 0) < 4
    table = jnp.where(first, jnp.cos(angles), jnp.sin(angles))
    for d in range(3):
        table_ref[d] = MOVES[d](table)

    def rows_of(group, carry):
        rows = pl.ds(pl.multiple_of(group * 16, 16), 16)
        for d in range(3):
            for out_colour in range(3):
                real_base = jnp.zeros((16, SITES), jnp.float32)
                imag_base = jnp.zeros((16, SITES), jnp.float32)
                for colour in range(3):
                    at = 2 * SITES * colour
                    real_vec = block_ref[rows, at : at + SITES].astype(jnp.float32)
                    imag_vec = block_ref[rows, at + SITES : at + 2 * SITES].astype(jnp.float32)
                    real_link = link_ref[d, colour, out_colour, 0]
                    imag_link = link_ref[d, colour, out_colour, 1]
                    real_base += real_vec * real_link + imag_vec * imag_link
                    imag_base += real_vec * imag_link - imag_vec * real_link
                real_base, imag_base = MOVES[d](real_base), MOVES[d](imag_base)
                at = 2 * SITES * out_colour
                to_ref, to = (raised_ref, 0) if d == 2 else (left_ref, 4 * d)
                for p in range(4):
                    cosine = table_ref[d, p : p + 1, :]
                    sine = table_ref[d, p + 4 : p + 5, :]
                    to_ref[to + p, rows, at : at + SITES] = (
                        real_base * cosine + imag_base * sine
                    ).astype(jnp.bfloat16)
                    to_ref[to + p, rows, at + SITES : at + 2 * SITES] = (
                        imag_base * cosine - real_base * sine
                    ).astype(jnp.bfloat16)
        return carry

    lax.fori_loop(0, ROWS // 16, rows_of, 0)


def left_operand(plane, block, links):
    return pl.pallas_call(
        left_kernel,
        out_shape=[
            jax.ShapeDtypeStruct((8, ROWS, DEPTH), jnp.bfloat16),
            jax.ShapeDtypeStruct((4, ROWS, DEPTH), jnp.bfloat16),
        ],
        in_specs=[pl.BlockSpec(memory_space=pltpu.SMEM)]
        + [pl.BlockSpec(memory_space=pltpu.VMEM)] * 2,
        out_specs=[pl.BlockSpec(memory_space=pltpu.VMEM)] * 2,
        scratch_shapes=[pltpu.VMEM((3, 8, SITES), jnp.float32)],
        compiler_params=pltpu.CompilerParams(vmem_limit_bytes=VMEM_BYTES),
    )(plane, block, links)


def product_kernel(half_ref, left_ref, raised_ref, near_ref, far_ref, out_ref, both_ref):
    def spread(source_ref, to):
        real_rows, imag_rows = slice(to, to + 128), slice(to + 256, to + 384)
        for colour in range(3):
            at = 2 * SITES * colour
            real_vec = source_ref[:, at : at + SITES]
            imag_vec = source_ref[:, at + SITES : at + 2 * SITES]
            both_ref[real_rows, at : at + SITES] = real_vec
            both_ref[real_rows, at + SITES : at + 2 * SITES] = -imag_vec
            both_ref[imag_rows, at : at + SITES] = imag_vec
            both_ref[imag_rows, at + SITES : at + 2 * SITES] = real_vec

    def multiply(source_ref, least, most):
        product = lax.dot_general(
            both_ref[...],
            source_ref[...],
            (((1,), (1,)), ((), ())),
            preferred_element_type=jnp.float32,
        )
        width = most - least
        real_part = product[0:256].reshape(32, 8, width)
        imag_part = product[256:512].reshape(32, 8, width)
        upper = lax.broadcasted_iota(jnp.int32, (32, 8, width), 1) < 4
        even = jnp.where(upper, real_part, pltpu.roll(imag_part, 4, 1)).astype(jnp.bfloat16)
        odd = jnp.where(upper, pltpu.roll(real_part, 4, 1), imag_part).astype(jnp.bfloat16)
        for block in range(8):
            near = block < 4
            half = half_ref[0] if near else 1 - half_ref[0]
            place = NEAR_ORDER[block] if near else block - 4
            for pair in range(4):
                out_ref[place, half, 2 * pair, :, least:most] = even[4 * block + pair]
                out_ref[place, half, 2 * pair + 1, :, least:most] = odd[4 * block + pair]

    spread(near_ref, 0)
    spread(far_ref, 128)
    multiply(left_ref, 0, 8 * ROWS)
    multiply(raised_ref, 8 * ROWS, 12 * ROWS)


def products(half, left, raised, near, far):
    return pl.pallas_call(
        product_kernel,
        out_shape=jax.ShapeDtypeStruct((4, 2, 8, 8, 12 * ROWS), jnp.bfloat16),
        in_specs=[pl.BlockSpec(memory_space=pltpu.SMEM)]
        + [pl.BlockSpec(memory_space=pltpu.VMEM)] * 4,
        out_specs=pl.BlockSpec(memory_space=pltpu.VMEM),
        scratch_shapes=[pltpu.VMEM((512, DEPTH), jnp.bfloat16)],
        compiler_params=pltpu.CompilerParams(vmem_limit_bytes=VMEM_BYTES),
    )(half, left, raised, near, far)


def body(eigenvectors, gauge_links, momenta):
    space = lax.axis_size("space")
    eig = lax.axis_size("eig")
    s = lax.axis_index("space")
    e = lax.axis_index("eig")
    block = eigenvectors.reshape(ROWS, DEPTH)
    row = lax.broadcasted_iota(jnp.int32, (5, 3), 0)
    column = lax.broadcasted_iota(jnp.int32, (5, 3), 1)
    plane = jnp.where(column == 0, s, space).astype(jnp.int32)
    plane = jnp.where(row < 4, jnp.pad(momenta, ((0, 1), (0, 0))), plane)
    half = (e & 1).astype(jnp.int32).reshape(1)
    groups = [list(range(0, eig, 2)), list(range(1, eig, 2))]

    partner = lax.ppermute(block, "eig", [(a, a ^ 1) for a in range(eig)])
    copies = jnp.pad(block, ((0, 0), (0, PAD)))
    copies = jnp.broadcast_to(copies[None], (eig // 2, ROWS, DEPTH + PAD))
    near_groups = [[2 * x + h for x in NEAR_ORDER] for h in range(2)]
    near = lax.all_to_all(
        copies, "eig", split_axis=0, concat_axis=0, axis_index_groups=near_groups, tiled=True
    ).reshape(eig // 2 * ROWS, DEPTH + PAD)
    left, raised = left_operand(plane, block, gauge_links)

    partner, left, raised = lax.optimization_barrier((partner, left, raised))
    raised = lax.ppermute(raised, "space", [(a, (a + 1) % space) for a in range(space)])
    far = lax.all_gather(partner, "eig", axis_index_groups=groups, tiled=True)
    left, raised = left.reshape(8 * ROWS, DEPTH), raised.reshape(4 * ROWS, DEPTH)
    chunks = products(half, left, raised, near, far).reshape(space, 8, 12 * ROWS)
    got = lax.all_to_all(chunks, "space", split_axis=0, concat_axis=0, tiled=True)
    total = jnp.sum(got.astype(jnp.float32), axis=0)
    return total.reshape(2, 4, 3, 4, ROWS).transpose(2, 3, 0, 4, 1)


def solution(mesh):
    return jax.shard_map(
        body,
        mesh=mesh,
        in_specs=(
            P("eig", None, None, "space", None),
            P(None, None, None, None, "space", None),
            P(),
        ),
        out_specs=P(None, None, None, "eig", "space"),
        check_vma=False,
    )
```

```python
import math

import jax
import jax.numpy as jnp
from jax import lax
from jax.experimental import pallas as pl
from jax.experimental.pallas import tpu as pltpu
from jax.sharding import PartitionSpec as P

LX = 64
LY = 8
SITES = LX * LY
ROWS = 32
DEPTH = 6 * SITES
PAD = 1024
NEAR_ORDER = (2, 0, 3, 1)
VMEM_BYTES = 40 * 1024 * 1024


def moved_across(field):
    lane = lax.broadcasted_iota(jnp.int32, field.shape, 1)
    return jnp.where(
        lane % LX == 0, pltpu.roll(field, SITES - LX + 1, 1), pltpu.roll(field, 1, 1)
    )


def moved_along(field):
    return pltpu.roll(field, LX, 1)


MOVES = (moved_across, moved_along, lambda field: field)


def left_kernel(plane_ref, block_ref, link_ref, left_ref, raised_ref, table_ref):
    row = lax.broadcasted_iota(jnp.int32, (8, SITES), 0) % 4
    site = lax.broadcasted_iota(jnp.int32, (8, SITES), 1)

    def component(k):
        value = jnp.full((8, SITES), plane_ref[3, k], jnp.int32)
        for p in range(3):
            value = jnp.where(row == p, plane_ref[p, k], value)
        return value

    x_frac = ((component(0) * (site % LX)) & (LX - 1)).astype(jnp.float32) / LX
    y_frac = ((component(1) * (site // LX)) & (LY - 1)).astype(jnp.float32) / LY
    extent = plane_ref[4, 1]
    z_frac = ((component(2) * plane_ref[4, 0]) & (extent - 1)).astype(jnp.float32)
    z_frac = z_frac / extent.astype(jnp.float32)
    angles = 2.0 * math.pi * (x_frac + y_frac + z_frac)
    first = lax.broadcasted_iota(jnp.int32, (8, SITES), 0) < 4
    table = jnp.where(first, jnp.cos(angles), jnp.sin(angles))
    for d in range(3):
        table_ref[d] = MOVES[d](table)

    def rows_of(group, carry):
        rows = pl.ds(pl.multiple_of(group * 16, 16), 16)
        for d in range(3):
            for out_colour in range(3):
                real_base = jnp.zeros((16, SITES), jnp.float32)
                imag_base = jnp.zeros((16, SITES), jnp.float32)
                for colour in range(3):
                    at = 2 * SITES * colour
                    real_vec = block_ref[rows, at : at + SITES].astype(jnp.float32)
                    imag_vec = block_ref[rows, at + SITES : at + 2 * SITES].astype(jnp.float32)
                    real_link = link_ref[d, colour, out_colour, 0]
                    imag_link = link_ref[d, colour, out_colour, 1]
                    real_base += real_vec * real_link + imag_vec * imag_link
                    imag_base += real_vec * imag_link - imag_vec * real_link
                real_base, imag_base = MOVES[d](real_base), MOVES[d](imag_base)
                at = 2 * SITES * out_colour
                to_ref, to = (raised_ref, 0) if d == 2 else (left_ref, 4 * d)
                for p in range(4):
                    cosine = table_ref[d, p : p + 1, :]
                    sine = table_ref[d, p + 4 : p + 5, :]
                    to_ref[to + p, rows, at : at + SITES] = (
                        real_base * cosine + imag_base * sine
                    ).astype(jnp.bfloat16)
                    to_ref[to + p, rows, at + SITES : at + 2 * SITES] = (
                        imag_base * cosine - real_base * sine
                    ).astype(jnp.bfloat16)
        return carry

    lax.fori_loop(0, ROWS // 16, rows_of, 0)


def left_operand(plane, block, links):
    return pl.pallas_call(
        left_kernel,
        out_shape=[
            jax.ShapeDtypeStruct((8, ROWS, DEPTH), jnp.bfloat16),
            jax.ShapeDtypeStruct((4, ROWS, DEPTH), jnp.bfloat16),
        ],
        in_specs=[pl.BlockSpec(memory_space=pltpu.SMEM)]
        + [pl.BlockSpec(memory_space=pltpu.VMEM)] * 2,
        out_specs=[pl.BlockSpec(memory_space=pltpu.VMEM)] * 2,
        scratch_shapes=[pltpu.VMEM((3, 8, SITES), jnp.float32)],
        compiler_params=pltpu.CompilerParams(vmem_limit_bytes=VMEM_BYTES),
    )(plane, block, links)


def product_kernel(half_ref, left_ref, raised_ref, near_ref, far_ref, out_ref, both_ref):
    def spread(source_ref, to):
        real_rows, imag_rows = slice(to, to + 128), slice(to + 256, to + 384)
        for colour in range(3):
            at = 2 * SITES * colour
            real_vec = source_ref[:, at : at + SITES]
            imag_vec = source_ref[:, at + SITES : at + 2 * SITES]
            both_ref[real_rows, at : at + SITES] = real_vec
            both_ref[real_rows, at + SITES : at + 2 * SITES] = -imag_vec
            both_ref[imag_rows, at : at + SITES] = imag_vec
            both_ref[imag_rows, at + SITES : at + 2 * SITES] = real_vec

    def multiply(source_ref, least, most):
        product = lax.dot_general(
            both_ref[...],
            source_ref[...],
            (((1,), (1,)), ((), ())),
            preferred_element_type=jnp.float32,
        )
        width = most - least
        real_part = product[0:256].reshape(32, 8, width)
        imag_part = product[256:512].reshape(32, 8, width)
        upper = lax.broadcasted_iota(jnp.int32, (32, 8, width), 1) < 4
        even = jnp.where(upper, real_part, pltpu.roll(imag_part, 4, 1)).astype(jnp.bfloat16)
        odd = jnp.where(upper, pltpu.roll(real_part, 4, 1), imag_part).astype(jnp.bfloat16)
        for block in range(8):
            near = block < 4
            half = half_ref[0] if near else 1 - half_ref[0]
            place = NEAR_ORDER[block] if near else block - 4
            for pair in range(4):
                out_ref[place, half, 2 * pair, :, least:most] = even[4 * block + pair]
                out_ref[place, half, 2 * pair + 1, :, least:most] = odd[4 * block + pair]

    spread(near_ref, 0)
    spread(far_ref, 128)
    multiply(left_ref, 0, 8 * ROWS)
    multiply(raised_ref, 8 * ROWS, 12 * ROWS)


def products(half, left, raised, near, far):
    return pl.pallas_call(
        product_kernel,
        out_shape=jax.ShapeDtypeStruct((4, 2, 8, 8, 12 * ROWS), jnp.bfloat16),
        in_specs=[pl.BlockSpec(memory_space=pltpu.SMEM)]
        + [pl.BlockSpec(memory_space=pltpu.VMEM)] * 4,
        out_specs=pl.BlockSpec(memory_space=pltpu.VMEM),
        scratch_shapes=[pltpu.VMEM((512, DEPTH), jnp.bfloat16)],
        compiler_params=pltpu.CompilerParams(vmem_limit_bytes=VMEM_BYTES),
    )(half, left, raised, near, far)


def body(eigenvectors, gauge_links, momenta):
    space = lax.axis_size("space")
    eig = lax.axis_size("eig")
    s = lax.axis_index("space")
    e = lax.axis_index("eig")
    block = eigenvectors.reshape(ROWS, DEPTH)
    row = lax.broadcasted_iota(jnp.int32, (5, 3), 0)
    column = lax.broadcasted_iota(jnp.int32, (5, 3), 1)
    plane = jnp.where(column == 0, s, space).astype(jnp.int32)
    plane = jnp.where(row < 4, jnp.pad(momenta, ((0, 1), (0, 0))), plane)
    half = (e & 1).astype(jnp.int32).reshape(1)
    groups = [list(range(0, eig, 2)), list(range(1, eig, 2))]

    partner = lax.ppermute(block, "eig", [(a, a ^ 1) for a in range(eig)])
    copies = jnp.pad(block, ((0, 0), (0, PAD)))
    copies = jnp.broadcast_to(copies[None], (eig // 2, ROWS, DEPTH + PAD))
    near_groups = [[2 * x + h for x in NEAR_ORDER] for h in range(2)]
    near = lax.all_to_all(
        copies, "eig", split_axis=0, concat_axis=0, axis_index_groups=near_groups, tiled=True
    ).reshape(eig // 2 * ROWS, DEPTH + PAD)
    left, raised = left_operand(plane, block, gauge_links)

    partner, left, raised = lax.optimization_barrier((partner, left, raised))
    raised = lax.ppermute(raised, "space", [(a, (a + 1) % space) for a in range(space)])
    far = lax.all_gather(partner, "eig", axis_index_groups=groups, tiled=True)
    left, raised = left.reshape(8 * ROWS, DEPTH), raised.reshape(4 * ROWS, DEPTH)
    chunks = products(half, left, raised, near, far).reshape(space, 8, 12 * ROWS)
    got = lax.all_to_all(chunks, "space", split_axis=0, concat_axis=0, tiled=True)
    total = jnp.sum(got.astype(jnp.float32), axis=0)
    return total.reshape(2, 4, 3, 4, ROWS).transpose(2, 3, 0, 4, 1)


def solution(mesh):
    return jax.shard_map(
        body,
        mesh=mesh,
        in_specs=(
            P("eig", None, None, "space", None),
            P(None, None, None, None, "space", None),
            P(),
        ),
        out_specs=P(None, None, None, "eig", "space"),
        check_vma=False,
    )
```

```python
import math

import jax
import jax.numpy as jnp
from jax import lax
from jax.experimental import pallas as pl
from jax.experimental.pallas import tpu as pltpu
from jax.sharding import PartitionSpec as P

LX = 64
LY = 8
SITES = LX * LY
ROWS = 32
DEPTH = 6 * SITES
PAD = 1024
NEAR_ORDER = (0, 2, 1, 3)
VMEM_BYTES = 40 * 1024 * 1024


def moved_across(field):
    lane = lax.broadcasted_iota(jnp.int32, field.shape, 1)
    return jnp.where(
        lane % LX == 0, pltpu.roll(field, SITES - LX + 1, 1), pltpu.roll(field, 1, 1)
    )


def moved_along(field):
    return pltpu.roll(field, LX, 1)


MOVES = (moved_across, moved_along, lambda field: field)


def left_kernel(plane_ref, block_ref, link_ref, left_ref, raised_ref, table_ref):
    row = lax.broadcasted_iota(jnp.int32, (8, SITES), 0) % 4
    site = lax.broadcasted_iota(jnp.int32, (8, SITES), 1)

    def component(k):
        value = jnp.full((8, SITES), plane_ref[3, k], jnp.int32)
        for p in range(3):
            value = jnp.where(row == p, plane_ref[p, k], value)
        return value

    x_frac = ((component(0) * (site % LX)) & (LX - 1)).astype(jnp.float32) / LX
    y_frac = ((component(1) * (site // LX)) & (LY - 1)).astype(jnp.float32) / LY
    extent = plane_ref[4, 1]
    z_frac = ((component(2) * plane_ref[4, 0]) & (extent - 1)).astype(jnp.float32)
    z_frac = z_frac / extent.astype(jnp.float32)
    angles = 2.0 * math.pi * (x_frac + y_frac + z_frac)
    first = lax.broadcasted_iota(jnp.int32, (8, SITES), 0) < 4
    table = jnp.where(first, jnp.cos(angles), jnp.sin(angles))
    for d in range(3):
        table_ref[d] = MOVES[d](table)

    def rows_of(group, carry):
        rows = pl.ds(pl.multiple_of(group * 16, 16), 16)
        for d in range(3):
            for out_colour in range(3):
                real_base = jnp.zeros((16, SITES), jnp.float32)
                imag_base = jnp.zeros((16, SITES), jnp.float32)
                for colour in range(3):
                    at = 2 * SITES * colour
                    real_vec = block_ref[rows, at : at + SITES].astype(jnp.float32)
                    imag_vec = block_ref[rows, at + SITES : at + 2 * SITES].astype(jnp.float32)
                    real_link = link_ref[d, colour, out_colour, 0]
                    imag_link = link_ref[d, colour, out_colour, 1]
                    real_base += real_vec * real_link + imag_vec * imag_link
                    imag_base += real_vec * imag_link - imag_vec * real_link
                real_base, imag_base = MOVES[d](real_base), MOVES[d](imag_base)
                at = 2 * SITES * out_colour
                to_ref, to = (raised_ref, 0) if d == 2 else (left_ref, 4 * d)
                for p in range(4):
                    cosine = table_ref[d, p : p + 1, :]
                    sine = table_ref[d, p + 4 : p + 5, :]
                    to_ref[to + p, rows, at : at + SITES] = (
                        real_base * cosine + imag_base * sine
                    ).astype(jnp.bfloat16)
                    to_ref[to + p, rows, at + SITES : at + 2 * SITES] = (
                        imag_base * cosine - real_base * sine
                    ).astype(jnp.bfloat16)
        return carry

    lax.fori_loop(0, ROWS // 16, rows_of, 0)


def left_operand(plane, block, links):
    return pl.pallas_call(
        left_kernel,
        out_shape=[
            jax.ShapeDtypeStruct((8, ROWS, DEPTH), jnp.bfloat16),
            jax.ShapeDtypeStruct((4, ROWS, DEPTH), jnp.bfloat16),
        ],
        in_specs=[pl.BlockSpec(memory_space=pltpu.SMEM)]
        + [pl.BlockSpec(memory_space=pltpu.VMEM)] * 2,
        out_specs=[pl.BlockSpec(memory_space=pltpu.VMEM)] * 2,
        scratch_shapes=[pltpu.VMEM((3, 8, SITES), jnp.float32)],
        compiler_params=pltpu.CompilerParams(vmem_limit_bytes=VMEM_BYTES),
    )(plane, block, links)


def product_kernel(half_ref, left_ref, raised_ref, near_ref, far_ref, out_ref, both_ref):
    def spread(source_ref, to):
        real_rows, imag_rows = slice(to, to + 128), slice(to + 256, to + 384)
        for colour in range(3):
            at = 2 * SITES * colour
            real_vec = source_ref[:, at : at + SITES]
            imag_vec = source_ref[:, at + SITES : at + 2 * SITES]
            both_ref[real_rows, at : at + SITES] = real_vec
            both_ref[real_rows, at + SITES : at + 2 * SITES] = -imag_vec
            both_ref[imag_rows, at : at + SITES] = imag_vec
            both_ref[imag_rows, at + SITES : at + 2 * SITES] = real_vec

    def multiply(source_ref, least, most):
        product = lax.dot_general(
            both_ref[...],
            source_ref[...],
            (((1,), (1,)), ((), ())),
            preferred_element_type=jnp.float32,
        )
        width = most - least
        real_part = product[0:256].reshape(32, 8, width)
        imag_part = product[256:512].reshape(32, 8, width)
        upper = lax.broadcasted_iota(jnp.int32, (32, 8, width), 1) < 4
        even = jnp.where(upper, real_part, pltpu.roll(imag_part, 4, 1)).astype(jnp.bfloat16)
        odd = jnp.where(upper, pltpu.roll(real_part, 4, 1), imag_part).astype(jnp.bfloat16)
        for block in range(8):
            near = block < 4
            half = half_ref[0] if near else 1 - half_ref[0]
            place = NEAR_ORDER[block] if near else block - 4
            for pair in range(4):
                out_ref[place, half, 2 * pair, :, least:most] = even[4 * block + pair]
                out_ref[place, half, 2 * pair + 1, :, least:most] = odd[4 * block + pair]

    spread(near_ref, 0)
    spread(far_ref, 128)
    multiply(left_ref, 0, 8 * ROWS)
    multiply(raised_ref, 8 * ROWS, 12 * ROWS)


def products(half, left, raised, near, far):
    return pl.pallas_call(
        product_kernel,
        out_shape=jax.ShapeDtypeStruct((4, 2, 8, 8, 12 * ROWS), jnp.bfloat16),
        in_specs=[pl.BlockSpec(memory_space=pltpu.SMEM)]
        + [pl.BlockSpec(memory_space=pltpu.VMEM)] * 4,
        out_specs=pl.BlockSpec(memory_space=pltpu.VMEM),
        scratch_shapes=[pltpu.VMEM((512, DEPTH), jnp.bfloat16)],
        compiler_params=pltpu.CompilerParams(vmem_limit_bytes=VMEM_BYTES),
    )(half, left, raised, near, far)


def body(eigenvectors, gauge_links, momenta):
    space = lax.axis_size("space")
    eig = lax.axis_size("eig")
    s = lax.axis_index("space")
    e = lax.axis_index("eig")
    block = eigenvectors.reshape(ROWS, DEPTH)
    row = lax.broadcasted_iota(jnp.int32, (5, 3), 0)
    column = lax.broadcasted_iota(jnp.int32, (5, 3), 1)
    plane = jnp.where(column == 0, s, space).astype(jnp.int32)
    plane = jnp.where(row < 4, jnp.pad(momenta, ((0, 1), (0, 0))), plane)
    half = (e & 1).astype(jnp.int32).reshape(1)
    groups = [list(range(0, eig, 2)), list(range(1, eig, 2))]

    partner = lax.ppermute(block, "eig", [(a, a ^ 1) for a in range(eig)])
    copies = jnp.pad(block, ((0, 0), (0, PAD)))
    copies = jnp.broadcast_to(copies[None], (eig // 2, ROWS, DEPTH + PAD))
    near_groups = [[2 * x + h for x in NEAR_ORDER] for h in range(2)]
    near = lax.all_to_all(
        copies, "eig", split_axis=0, concat_axis=0, axis_index_groups=near_groups, tiled=True
    ).reshape(eig // 2 * ROWS, DEPTH + PAD)
    left, raised = left_operand(plane, block, gauge_links)

    partner, left, raised = lax.optimization_barrier((partner, left, raised))
    raised = lax.ppermute(raised, "space", [(a, (a + 1) % space) for a in range(space)])
    far = lax.all_gather(partner, "eig", axis_index_groups=groups, tiled=True)
    left, raised = left.reshape(8 * ROWS, DEPTH), raised.reshape(4 * ROWS, DEPTH)
    chunks = products(half, left, raised, near, far).reshape(space, 8, 12 * ROWS)
    got = lax.all_to_all(chunks, "space", split_axis=0, concat_axis=0, tiled=True)
    total = jnp.sum(got.astype(jnp.float32), axis=0)
    return total.reshape(2, 4, 3, 4, ROWS).transpose(2, 3, 0, 4, 1)


def solution(mesh):
    return jax.shard_map(
        body,
        mesh=mesh,
        in_specs=(
            P("eig", None, None, "space", None),
            P(None, None, None, None, "space", None),
            P(),
        ),
        out_specs=P(None, None, None, "eig", "space"),
        check_vma=False,
    )
```

```python
import math

import jax
import jax.numpy as jnp
from jax import lax
from jax.experimental import pallas as pl
from jax.experimental.pallas import tpu as pltpu
from jax.sharding import PartitionSpec as P

LX = 64
LY = 8
SITES = LX * LY
ROWS = 32
DEPTH = 6 * SITES
PAD = 1024
NEAR_ORDER = (3, 1, 2, 0)
VMEM_BYTES = 40 * 1024 * 1024


def moved_across(field):
    lane = lax.broadcasted_iota(jnp.int32, field.shape, 1)
    return jnp.where(
        lane % LX == 0, pltpu.roll(field, SITES - LX + 1, 1), pltpu.roll(field, 1, 1)
    )


def moved_along(field):
    return pltpu.roll(field, LX, 1)


MOVES = (moved_across, moved_along, lambda field: field)


def left_kernel(plane_ref, block_ref, link_ref, left_ref, raised_ref, table_ref):
    row = lax.broadcasted_iota(jnp.int32, (8, SITES), 0) % 4
    site = lax.broadcasted_iota(jnp.int32, (8, SITES), 1)

    def component(k):
        value = jnp.full((8, SITES), plane_ref[3, k], jnp.int32)
        for p in range(3):
            value = jnp.where(row == p, plane_ref[p, k], value)
        return value

    x_frac = ((component(0) * (site % LX)) & (LX - 1)).astype(jnp.float32) / LX
    y_frac = ((component(1) * (site // LX)) & (LY - 1)).astype(jnp.float32) / LY
    extent = plane_ref[4, 1]
    z_frac = ((component(2) * plane_ref[4, 0]) & (extent - 1)).astype(jnp.float32)
    z_frac = z_frac / extent.astype(jnp.float32)
    angles = 2.0 * math.pi * (x_frac + y_frac + z_frac)
    first = lax.broadcasted_iota(jnp.int32, (8, SITES), 0) < 4
    table = jnp.where(first, jnp.cos(angles), jnp.sin(angles))
    for d in range(3):
        table_ref[d] = MOVES[d](table)

    def rows_of(group, carry):
        rows = pl.ds(pl.multiple_of(group * 16, 16), 16)
        for d in range(3):
            for out_colour in range(3):
                real_base = jnp.zeros((16, SITES), jnp.float32)
                imag_base = jnp.zeros((16, SITES), jnp.float32)
                for colour in range(3):
                    at = 2 * SITES * colour
                    real_vec = block_ref[rows, at : at + SITES].astype(jnp.float32)
                    imag_vec = block_ref[rows, at + SITES : at + 2 * SITES].astype(jnp.float32)
                    real_link = link_ref[d, colour, out_colour, 0]
                    imag_link = link_ref[d, colour, out_colour, 1]
                    real_base += real_vec * real_link + imag_vec * imag_link
                    imag_base += real_vec * imag_link - imag_vec * real_link
                real_base, imag_base = MOVES[d](real_base), MOVES[d](imag_base)
                at = 2 * SITES * out_colour
                to_ref, to = (raised_ref, 0) if d == 2 else (left_ref, 4 * d)
                for p in range(4):
                    cosine = table_ref[d, p : p + 1, :]
                    sine = table_ref[d, p + 4 : p + 5, :]
                    to_ref[to + p, rows, at : at + SITES] = (
                        real_base * cosine + imag_base * sine
                    ).astype(jnp.bfloat16)
                    to_ref[to + p, rows, at + SITES : at + 2 * SITES] = (
                        imag_base * cosine - real_base * sine
                    ).astype(jnp.bfloat16)
        return carry

    lax.fori_loop(0, ROWS // 16, rows_of, 0)


def left_operand(plane, block, links):
    return pl.pallas_call(
        left_kernel,
        out_shape=[
            jax.ShapeDtypeStruct((8, ROWS, DEPTH), jnp.bfloat16),
            jax.ShapeDtypeStruct((4, ROWS, DEPTH), jnp.bfloat16),
        ],
        in_specs=[pl.BlockSpec(memory_space=pltpu.SMEM)]
        + [pl.BlockSpec(memory_space=pltpu.VMEM)] * 2,
        out_specs=[pl.BlockSpec(memory_space=pltpu.VMEM)] * 2,
        scratch_shapes=[pltpu.VMEM((3, 8, SITES), jnp.float32)],
        compiler_params=pltpu.CompilerParams(vmem_limit_bytes=VMEM_BYTES),
    )(plane, block, links)


def product_kernel(half_ref, left_ref, raised_ref, near_ref, far_ref, out_ref, both_ref):
    def spread(source_ref, to):
        real_rows, imag_rows = slice(to, to + 128), slice(to + 256, to + 384)
        for colour in range(3):
            at = 2 * SITES * colour
            real_vec = source_ref[:, at : at + SITES]
            imag_vec = source_ref[:, at + SITES : at + 2 * SITES]
            both_ref[real_rows, at : at + SITES] = real_vec
            both_ref[real_rows, at + SITES : at + 2 * SITES] = -imag_vec
            both_ref[imag_rows, at : at + SITES] = imag_vec
            both_ref[imag_rows, at + SITES : at + 2 * SITES] = real_vec

    def multiply(source_ref, least, most):
        product = lax.dot_general(
            both_ref[...],
            source_ref[...],
            (((1,), (1,)), ((), ())),
            preferred_element_type=jnp.float32,
        )
        width = most - least
        real_part = product[0:256].reshape(32, 8, width)
        imag_part = product[256:512].reshape(32, 8, width)
        upper = lax.broadcasted_iota(jnp.int32, (32, 8, width), 1) < 4
        even = jnp.where(upper, real_part, pltpu.roll(imag_part, 4, 1)).astype(jnp.bfloat16)
        odd = jnp.where(upper, pltpu.roll(real_part, 4, 1), imag_part).astype(jnp.bfloat16)
        for block in range(8):
            near = block < 4
            half = half_ref[0] if near else 1 - half_ref[0]
            place = NEAR_ORDER[block] if near else block - 4
            for pair in range(4):
                out_ref[place, half, 2 * pair, :, least:most] = even[4 * block + pair]
                out_ref[place, half, 2 * pair + 1, :, least:most] = odd[4 * block + pair]

    spread(near_ref, 0)
    spread(far_ref, 128)
    multiply(left_ref, 0, 8 * ROWS)
    multiply(raised_ref, 8 * ROWS, 12 * ROWS)


def products(half, left, raised, near, far):
    return pl.pallas_call(
        product_kernel,
        out_shape=jax.ShapeDtypeStruct((4, 2, 8, 8, 12 * ROWS), jnp.bfloat16),
        in_specs=[pl.BlockSpec(memory_space=pltpu.SMEM)]
        + [pl.BlockSpec(memory_space=pltpu.VMEM)] * 4,
        out_specs=pl.BlockSpec(memory_space=pltpu.VMEM),
        scratch_shapes=[pltpu.VMEM((512, DEPTH), jnp.bfloat16)],
        compiler_params=pltpu.CompilerParams(vmem_limit_bytes=VMEM_BYTES),
    )(half, left, raised, near, far)


def body(eigenvectors, gauge_links, momenta):
    space = lax.axis_size("space")
    eig = lax.axis_size("eig")
    s = lax.axis_index("space")
    e = lax.axis_index("eig")
    block = eigenvectors.reshape(ROWS, DEPTH)
    row = lax.broadcasted_iota(jnp.int32, (5, 3), 0)
    column = lax.broadcasted_iota(jnp.int32, (5, 3), 1)
    plane = jnp.where(column == 0, s, space).astype(jnp.int32)
    plane = jnp.where(row < 4, jnp.pad(momenta, ((0, 1), (0, 0))), plane)
    half = (e & 1).astype(jnp.int32).reshape(1)
    groups = [list(range(0, eig, 2)), list(range(1, eig, 2))]

    partner = lax.ppermute(block, "eig", [(a, a ^ 1) for a in range(eig)])
    copies = jnp.pad(block, ((0, 0), (0, PAD)))
    copies = jnp.broadcast_to(copies[None], (eig // 2, ROWS, DEPTH + PAD))
    near_groups = [[2 * x + h for x in NEAR_ORDER] for h in range(2)]
    near = lax.all_to_all(
        copies, "eig", split_axis=0, concat_axis=0, axis_index_groups=near_groups, tiled=True
    ).reshape(eig // 2 * ROWS, DEPTH + PAD)
    left, raised = left_operand(plane, block, gauge_links)

    partner, left, raised = lax.optimization_barrier((partner, left, raised))
    raised = lax.ppermute(raised, "space", [(a, (a + 1) % space) for a in range(space)])
    far = lax.all_gather(partner, "eig", axis_index_groups=groups, tiled=True)
    left, raised = left.reshape(8 * ROWS, DEPTH), raised.reshape(4 * ROWS, DEPTH)
    chunks = products(half, left, raised, near, far).reshape(space, 8, 12 * ROWS)
    got = lax.all_to_all(chunks, "space", split_axis=0, concat_axis=0, tiled=True)
    total = jnp.sum(got.astype(jnp.float32), axis=0)
    return total.reshape(2, 4, 3, 4, ROWS).transpose(2, 3, 0, 4, 1)


def solution(mesh):
    return jax.shard_map(
        body,
        mesh=mesh,
        in_specs=(
            P("eig", None, None, "space", None),
            P(None, None, None, None, "space", None),
            P(),
        ),
        out_specs=P(None, None, None, "eig", "space"),
        check_vma=False,
    )
```
